128 devices in a mesh: seq: 32 (over x, y, core), head: 4 (over z).
Axes of the slice: x: 4, y: 4, z: 4, core: 2. Of those that a mesh axis runs over, the one named last changes fastest.
Arguments:
- clip_tokens: bfloat16 [4096, 5120], P(('seq', 'head')), may hold values from -11 to 11
- w_qkv: bfloat16 [3, 5120, 2560], P(None, None, 'head'), may hold values from -1 to 1
- readout: bfloat16 [4096, 2560], P('seq', 'head'), may hold values from -6 to 6
- token_latent_frame: int32 [4096], replicated, may hold values from 0 to 7, never falling along the last dimension, each value on 1 to 1024 neighbouring positions
- frame_mask: int32 [8, 8], replicated, may hold values from 0 to 1, as said below
Outputs:
- grad_x: bfloat16 [4096, 5120], P(('seq', 'head'))
- penalty_grad: bfloat16 [4096, 2560], P('seq', 'head')
The draws below stay inside these ranges and needn't reach their ends.
Inputs may be any that keep to these rules, and one draw needn't show every extreme that they name: `token_latent_frame`: frames never fall along the tokens; each frame holds 1 to 1024 tokens, one exactly that many. `frame_mask`: entry (i, j) is 1 where tokens of frame i attend to tokens of frame j; it is 1 wherever i and j differ by at most one, and some farther pairs are 1 as well.
All inputs are finite; a program needn't handle non-finite values.
Results may differ from the reference program's by a relative error of at most 0.03.
The reference program's roundings to bfloat16 on the way count: a program that leaves them out, or rounds other values in their place, can miss the bound.
Values may be sent and summed in bfloat16 or wider, within the bound.
A program may use at most 192 MiB of HBM per device.

```python
import math
import jax
import jax.numpy as jnp
import numpy as np
from jax import lax

D = 5120
HD = 128
HEADS = 20
FRAMES = 8
TOK_DEV = 128
TOKENS = 4096
N_SEQ = 32


def draw_clip_tokens(key, part):
    first_key = jax.random.fold_in(key, 0)
    result = jnp.clip(jax.random.normal(first_key, (TOKENS, D), jnp.float32), -6.0, 6.0)
    return result.astype(jnp.bfloat16)


def draw_w_qkv(key, part):
    noise = jnp.clip(jax.random.normal(key, (3, D, HEADS * HD), jnp.float32), -5.0, 5.0) * D ** (-0.5)
    result = noise
    return result.astype(jnp.bfloat16)


def draw_frame_mask(key, part):
    far_draw = jax.random.randint(key, (FRAMES, FRAMES), 0, 4)
    row_ids = jnp.arange(FRAMES, dtype=jnp.int32)[:, None]
    col_ids = jnp.arange(FRAMES, dtype=jnp.int32)[None, :]
    frame_gap = jnp.abs(row_ids - col_ids)
    return jnp.where((frame_gap <= 1) | (far_draw * frame_gap < 4), 1, 0).astype(jnp.int32)


def steps_of(rng, shape, shards, low, largest):
    factor_of, own = 1.0, jax.random.fold_in(rng, 6)
    for position, parts in shards:
        draws = jnp.exp(jax.random.uniform(jax.random.fold_in(own, position), (parts,), jnp.float32, low / len(shards), largest / len(shards)))
        factor_of = factor_of * jnp.repeat(draws, shape[position] // parts).reshape([-1 if axis == position else 1 for axis in range(len(shape))])
    return factor_of


def profile(count, total, reach, slope):
    loads = [(1 << 20) // math.isqrt(rank ** slope) + 1 for rank in range(2, count + 1)]
    surplus, holding = total - reach - (count - 1), [1] * (count - 1)
    while surplus > 0:
        candidates = [i for i in range(count - 1) if holding[i] < reach]
        whole, left = sum([loads[i] for i in candidates]), surplus
        for i in candidates:
            addition = min(reach - holding[i], max(1, left * loads[i] // whole), surplus)
            holding[i] = holding[i] + addition
            surplus = surplus - addition
    return np.array([reach] + holding)


def uneven_parts(rng, count, total, limit, slope):
    if count == 2:
        one = jax.random.randint(rng, (), max(1, total - limit), min(limit, total - 1) + 1)
        return jnp.stack([one, total - one])
    sizes = jnp.asarray(profile(count, total, limit, slope), jnp.int32)
    twos = (count - 1) // 2
    source_of, taker = sizes[1:1 + 2 * twos:2], sizes[2:2 + 2 * twos:2]
    margin = jnp.minimum(source_of - 1, limit - taker)
    passed = jax.random.randint(jax.random.fold_in(rng, 1), (twos,), 0, 1 << 20) % (margin + 1)
    sizes = sizes.at[1:1 + 2 * twos:2].set(source_of - passed).at[2:2 + 2 * twos:2].set(taker + passed)
    return sizes[jax.random.permutation(jax.random.fold_in(rng, 2), count)]


def normal_values(own_key, shape, scale, bound, shards=(), kind=jnp.bfloat16):
    values = scale * jax.random.normal(own_key, shape, jnp.float32)
    if shards:
        values = values * steps_of(own_key, shape, shards, -0.22, 0.18)
    return jnp.clip(values, -bound, bound).astype(kind)


def setup_inputs(seed: int = 0) -> dict:
    streams_of = jax.random.split(jax.random.key(seed), 6)
    clip_tokens = draw_clip_tokens(jax.random.fold_in(streams_of[5], 71), 0)
    w_qkv = draw_w_qkv(jax.random.fold_in(streams_of[5], 71), 0)
    readout = normal_values(streams_of[2], (TOKENS, HEADS * HD), 1.0, 6.0, ((0, 32), (1, 4)))
    token_latent_frame = jnp.searchsorted(jnp.cumsum(uneven_parts(streams_of[3], FRAMES, TOKENS, TOKENS // 4, 1)), jnp.arange(TOKENS), side="right").astype(jnp.int32)
    frame_mask = draw_frame_mask(jax.random.fold_in(streams_of[5], 71), 0)
    return dict(clip_tokens=clip_tokens, w_qkv=w_qkv, readout=readout, token_latent_frame=token_latent_frame, frame_mask=frame_mask)


masked_value = -1e30


def reference(clip_tokens, w_qkv, readout, token_latent_frame, frame_mask):
    score_scale = HD ** -0.5

    def project(inputs, which):
        return jnp.dot(inputs, w_qkv[which], preferred_element_type=jnp.float32).astype(jnp.bfloat16)

    queries = project(clip_tokens, 0)
    keys_all = project(clip_tokens, 1)
    values_all = project(clip_tokens, 2)
    allowed = frame_mask[token_latent_frame][:, token_latent_frame] == 1

    def by_head(array):
        return array.reshape(TOKENS, HEADS, HD).transpose(1, 0, 2)

    def to_rows(array):
        return array.transpose(1, 0, 2).reshape(TOKENS, HEADS * HD)

    def weights_of(query_head, key_head):
        raw = jnp.dot(query_head, key_head.T, preferred_element_type=jnp.float32) * score_scale
        logits = jnp.where(allowed, raw, masked_value)
        row_max = logits.max(axis=1, keepdims=True)
        row_sum = jnp.where(allowed, jnp.exp(logits - row_max), 0.0).sum(axis=1, keepdims=True)
        log_norm = row_max + jnp.log(row_sum)
        return jnp.where(allowed, jnp.exp(logits - log_norm), 0.0)

    def block_sums(left_side, right_side, penalty_factor):
        leading_blocks = left_side.reshape(N_SEQ, TOK_DEV, TOKENS).astype(jnp.float32)
        trailing_blocks = right_side.reshape(N_SEQ, TOK_DEV, HD).astype(jnp.float32)
        part_list = (penalty_factor * jnp.einsum("frv,frp->fvp", leading_blocks, trailing_blocks)).astype(jnp.bfloat16)
        part_list = lax.optimization_barrier(part_list)
        return part_list.astype(jnp.float32).sum(axis=0)

    def head_grads(operands):
        query_head, key_head, value_head, readout_head = operands
        weights = weights_of(query_head, key_head)
        readout_dots = jnp.dot(readout_head, value_head.T, preferred_element_type=jnp.float32)
        row_dots = (weights * readout_dots).sum(axis=1, keepdims=True)
        logit_grads = (weights * (readout_dots - row_dots)).astype(jnp.bfloat16)
        weights_low = weights.astype(jnp.bfloat16)
        query_grad = score_scale * jnp.dot(logit_grads, key_head, preferred_element_type=jnp.float32)
        key_grad = block_sums(logit_grads, query_head, score_scale)
        value_grad = block_sums(weights_low, readout_head, 1.0)
        return query_grad, key_grad, value_grad

    grads = lax.map(head_grads, (by_head(queries), by_head(keys_all), by_head(values_all), by_head(readout)))
    stacked = jnp.stack([to_rows(grad_part) for grad_part in grads]).astype(jnp.bfloat16)
    grad_x = jnp.einsum("cte,cde->td", stacked.astype(jnp.float32), w_qkv.astype(jnp.float32)).astype(jnp.bfloat16)

    query_dot = project(grad_x, 0)
    key_dot = project(grad_x, 1)
    value_dot = project(grad_x, 2)

    def head_tangent(operands):
        query_head, key_head, value_head, query_tangent, key_tangent, value_tangent = operands
        weights = weights_of(query_head, key_head)
        logit_dots = (jnp.dot(query_tangent, key_head.T, preferred_element_type=jnp.float32)
                      + jnp.dot(query_head, key_tangent.T, preferred_element_type=jnp.float32)) * score_scale
        curve_terms = weights * logit_dots
        curve = curve_terms.sum(axis=1, keepdims=True)
        weights_low = weights.astype(jnp.bfloat16)
        combined = (jnp.dot(curve_terms.astype(jnp.bfloat16), value_head, preferred_element_type=jnp.float32)
                    + jnp.dot(weights_low, value_tangent, preferred_element_type=jnp.float32))
        plain_sum = jnp.dot(weights_low, value_head, preferred_element_type=jnp.float32)
        return combined - curve * plain_sum

    tangent_out = lax.map(head_tangent, (by_head(queries), by_head(keys_all), by_head(values_all),
                                         by_head(query_dot), by_head(key_dot), by_head(value_dot)))
    penalty_grad = to_rows(tangent_out).astype(jnp.bfloat16)
    return grad_x, penalty_grad
```

```python
import functools
import math

import jax
import jax.numpy as jnp
from jax import lax
from jax.experimental import pallas as pl
from jax.experimental.pallas import tpu as pltpu
from jax.sharding import PartitionSpec as P

HD = 128
MESH = pl.DeviceIdType.MESH
LOG2E = math.log2(math.e)
BARRED = -1e30

CHIPS = 16
BUSY = 15
HEADS = 5
SLOTS = 6


def start_of(third):
    return (CHIPS * third + 2) // 3


def third_of(chip):
    return (chip * 3) // CHIPS


def place():
    me = lax.axis_index("seq")
    return me // 2, me % 2


def enter(chip, core):
    barrier = pltpu.get_barrier_semaphore()

    def greet(step, carry):
        peer = (chip + step) % CHIPS
        pl.semaphore_signal(barrier, inc=1, device_id={"seq": 2 * peer + core}, device_id_type=MESH)
        return carry

    lax.fori_loop(1, CHIPS, greet, 0)
    pl.semaphore_signal(barrier, inc=1, device_id={"seq": 2 * chip + 1 - core}, device_id_type=MESH)
    pl.semaphore_wait(barrier, CHIPS)


def remote(src, dst, send_sem, recv_sem, device):
    return pltpu.make_async_remote_copy(
        src_ref=src,
        dst_ref=dst,
        send_sem=send_sem,
        recv_sem=recv_sem,
        device_id={"seq": device},
        device_id_type=MESH,
    )


def deal_kernel(kv_ref, q_ref, kv_out, q_out, kv_send, kv_recv, pass_send, pass_recv, q_send, q_recv):
    chip, core = place()
    partner = 2 * chip + 1 - core
    third = third_of(chip)
    slot = chip - start_of(third)
    enter(chip, core)

    def kv_copy(d):
        return remote(
            kv_ref.at[:, d // 3], kv_out.at[:, chip, core], kv_send.at[d], kv_recv.at[chip], 2 * d + core
        )

    def q_copy(h):
        return remote(q_ref.at[:, h], q_out.at[:, slot], q_send.at[h], q_recv.at[slot], 2 * (3 * h + third) + core)

    def own_kv():
        return pltpu.make_async_copy(kv_ref.at[:, chip // 3], kv_out.at[:, chip, core], kv_recv.at[chip])

    def own_q():
        return pltpu.make_async_copy(q_ref.at[:, chip // 3], q_out.at[:, slot], q_recv.at[slot])

    def send_q(h, carry):
        @pl.when(3 * h + third != chip)
        def _():
            q_copy(h).start()

        @pl.when(3 * h + third == chip)
        def _():
            own_q().start()

        return carry

    def send_kv(step, carry):
        d = (chip + step) % CHIPS

        @pl.when(jnp.logical_and(d < BUSY, step > 0))
        def _():
            kv_copy(d).start()

        @pl.when(jnp.logical_and(d < BUSY, step == 0))
        def _():
            own_kv().start()

        return carry

    lax.fori_loop(0, CHIPS, send_kv, 0)
    lax.fori_loop(0, HEADS, send_q, 0)

    own_third = chip % 3
    first = start_of(own_third)
    count = start_of(own_third + 1) - first

    def pass_copy(source):
        return remote(
            kv_out.at[:, source, core],
            kv_out.at[:, source, core],
            pass_send.at[source],
            pass_recv.at[source],
            partner,
        )

    def pass_wait(source):
        return remote(
            kv_out.at[:, source, 1 - core],
            kv_out.at[:, source, 1 - core],
            pass_send.at[source],
            pass_recv.at[source],
            partner,
        )

    @pl.when(chip < BUSY)
    def _():
        def arrive(step, carry):
            source = (chip + CHIPS - step) % CHIPS

            @pl.when(step > 0)
            def _():
                remote(
                    kv_ref.at[:, 0], kv_out.at[:, source, core], kv_send.at[0], kv_recv.at[source], partner
                ).wait_recv()

            @pl.when(step == 0)
            def _():
                own_kv().wait()

            pass_copy(source).start()
            return carry

        lax.fori_loop(0, CHIPS, arrive, 0)

        def arrive_q(n, carry):
            @pl.when(first + n != chip)
            def _():
                remote(q_ref.at[:, 0], q_out.at[:, n], q_send.at[0], q_recv.at[n], partner).wait_recv()

            @pl.when(first + n == chip)
            def _():
                own_q().wait()

            return carry

        lax.fori_loop(0, count, arrive_q, 0)

        @pl.when(count < SLOTS)
        def _():
            q_out[:, SLOTS - 1] = jnp.zeros_like(q_out[:, SLOTS - 1])

        def passed(step, carry):
            source = (chip + CHIPS - step) % CHIPS
            pass_wait(source).wait_recv()
            pass_copy(source).wait_send()
            return carry

        lax.fori_loop(0, CHIPS, passed, 0)

    def sent_kv(step, carry):
        d = (chip + step) % CHIPS

        @pl.when(d < BUSY)
        def _():
            kv_copy(d).wait_send()

        return carry

    lax.fori_loop(1, CHIPS, sent_kv, 0)

    def sent_q(h, carry):
        @pl.when(3 * h + third != chip)
        def _():
            q_copy(h).wait_send()

        return carry

    lax.fori_loop(0, HEADS, sent_q, 0)


VMEM = pl.BlockSpec(memory_space=pltpu.VMEM)
DMA = pltpu.SemaphoreType.DMA


def deal(kv, q, collective_id):
    parts = q.shape[0]
    return pl.pallas_call(
        deal_kernel,
        out_shape=(
            jax.ShapeDtypeStruct((2, CHIPS, 2, HD, HD), jnp.bfloat16),
            jax.ShapeDtypeStruct((parts, SLOTS, HD, HD), jnp.bfloat16),
        ),
        in_specs=[VMEM] * 2,
        out_specs=(VMEM, VMEM),
        scratch_shapes=[
            DMA((CHIPS,)),
            DMA((CHIPS,)),
            DMA((CHIPS,)),
            DMA((CHIPS,)),
            DMA((HEADS,)),
            DMA((SLOTS,)),
        ],
        compiler_params=pltpu.CompilerParams(
            collective_id=collective_id, has_side_effects=True, vmem_limit_bytes=32 << 20
        ),
        name="deal",
    )(kv, q)


def give_back(chip, core, src, dst, send, recv):
    own_third = chip % 3
    first = start_of(own_third)
    count = start_of(own_third + 1) - first
    third = third_of(chip)
    own_head = chip // 3

    def out_copy(n):
        return remote(src.at[n], dst.at[own_head], send.at[n], recv.at[own_head], 2 * (first + n) + core)

    def own():
        return pltpu.make_async_copy(src.at[chip - first], dst.at[own_head], recv.at[own_head])

    def begin():
        @pl.when(chip < BUSY)
        def _():
            def go(n, carry):
                @pl.when(first + n != chip)
                def _():
                    out_copy(n).start()

                @pl.when(first + n == chip)
                def _():
                    own().start()

                return carry

            lax.fori_loop(0, count, go, 0)

    def end():
        def come(h, carry):
            @pl.when(3 * h + third != chip)
            def _():
                remote(src.at[0], dst.at[h], send.at[0], recv.at[h], 2 * chip + 1 - core).wait_recv()

            @pl.when(3 * h + third == chip)
            def _():
                own().wait()

            return carry

        lax.fori_loop(0, HEADS, come, 0)

        @pl.when(chip < BUSY)
        def _():
            def gone(n, carry):
                @pl.when(first + n != chip)
                def _():
                    out_copy(n).wait_send()

                return carry

            lax.fori_loop(0, count, gone, 0)

    return begin, end


def return_kernel(dq_ref, q_out, q_send, q_recv):
    chip, core = place()
    enter(chip, core)
    begin, end = give_back(chip, core, dq_ref, q_out, q_send, q_recv)
    begin()
    end()


def return_queries(dq, collective_id):
    return pl.pallas_call(
        return_kernel,
        out_shape=jax.ShapeDtypeStruct((HEADS, HD, HD), jnp.bfloat16),
        in_specs=[VMEM],
        out_specs=VMEM,
        scratch_shapes=[DMA((SLOTS,)), DMA((HEADS,))],
        compiler_params=pltpu.CompilerParams(
            collective_id=collective_id, has_side_effects=True, vmem_limit_bytes=32 << 20
        ),
        name="return_queries",
    )(dq)


def reduce_kernel(
    dkv_ref, dq_ref, kv_sum, q_out, other, mixed, landed, x_send, x_recv, kv_send, kv_recv, q_send, q_recv
):
    chip, core = place()
    partner = 2 * chip + 1 - core
    enter(chip, core)
    begin, end = give_back(chip, core, dq_ref, q_out, q_send, q_recv)

    def swap(target):
        return remote(
            dkv_ref.at[:, target, 1 - core], other.at[:, target], x_send.at[target], x_recv.at[target], partner
        )

    def out_copy(target):
        return remote(
            mixed.at[:, target], landed.at[chip], kv_send.at[target], kv_recv.at[chip], 2 * target + core
        )

    def own():
        return pltpu.make_async_copy(mixed.at[:, chip], landed.at[chip], kv_recv.at[chip])

    @pl.when(chip < BUSY)
    def _():
        def start_swap(step, carry):
            swap((chip + step) % CHIPS).start()
            return carry

        lax.fori_loop(0, CHIPS, start_swap, 0)

    begin()

    @pl.when(chip < BUSY)
    def _():
        def mix(step, carry):
            target = (chip + step) % CHIPS
            swap(target).wait_recv()
            mixed[:, target] = (
                dkv_ref[:, target, core].astype(jnp.float32) + other[:, target].astype(jnp.float32)
            ).astype(jnp.bfloat16)

            @pl.when(step > 0)
            def _():
                out_copy(target).start()

            @pl.when(step == 0)
            def _():
                own().start()

            return carry

        lax.fori_loop(0, CHIPS, mix, 0)

    def come(step, carry):
        source = (chip + CHIPS - step) % CHIPS

        @pl.when(jnp.logical_and(source < BUSY, step > 0))
        def _():
            remote(
                mixed.at[:, 0], landed.at[source], kv_send.at[0], kv_recv.at[source], partner
            ).wait_recv()

        @pl.when(jnp.logical_and(source < BUSY, step == 0))
        def _():
            own().wait()

        return carry

    lax.fori_loop(0, CHIPS, come, 0)

    def add_up(h, carry):
        total = landed[3 * h].astype(jnp.float32) + landed[3 * h + 1].astype(jnp.float32)
        kv_sum[:, h] = (total + landed[3 * h + 2].astype(jnp.float32)).astype(jnp.bfloat16)
        return carry

    lax.fori_loop(0, HEADS, add_up, 0)
    end()

    @pl.when(chip < BUSY)
    def _():
        def gone(step, carry):
            target = (chip + step) % CHIPS
            swap(target).wait_send()

            @pl.when(step > 0)
            def _():
                out_copy(target).wait_send()

            return carry

        lax.fori_loop(0, CHIPS, gone, 0)


def reduce_back(dkv, dq, collective_id):
    return pl.pallas_call(
        reduce_kernel,
        out_shape=(
            jax.ShapeDtypeStruct((2, HEADS, HD, HD), jnp.bfloat16),
            jax.ShapeDtypeStruct((HEADS, HD, HD), jnp.bfloat16),
        ),
        in_specs=[VMEM] * 2,
        out_specs=(VMEM, VMEM),
        scratch_shapes=[
            pltpu.VMEM((2, CHIPS, HD, HD), jnp.bfloat16),
            pltpu.VMEM((2, CHIPS, HD, HD), jnp.bfloat16),
            pltpu.VMEM((CHIPS, 2, HD, HD), jnp.bfloat16),
            DMA((CHIPS,)),
            DMA((CHIPS,)),
            DMA((CHIPS,)),
            DMA((CHIPS,)),
            DMA((SLOTS,)),
            DMA((HEADS,)),
        ],
        compiler_params=pltpu.CompilerParams(
            collective_id=collective_id, has_side_effects=True, vmem_limit_bytes=32 << 20
        ),
        name="reduce_back",
    )(dkv, dq)


TOKENS = 4096
ROWS = SLOTS * HD
CHUNK = 256
SCALE = HD ** (-0.5)


def nt(left, right):
    return lax.dot_general(left, right, (((1,), (1,)), ((), ())), preferred_element_type=jnp.float32)


def nn(left, right):
    return lax.dot_general(left, right, (((1,), (0,)), ((), ())), preferred_element_type=jnp.float32)


def tn(left, right):
    return lax.dot_general(left, right, (((0,), (0,)), ((), ())), preferred_element_type=jnp.float32)


def rows_of(chunk):
    return pl.ds(pl.multiple_of(chunk * CHUNK, CHUNK), CHUNK)


def grads_kernel(kv_ref, qr_ref, key_hot, row_bar, dkv_ref, dq_ref, norm_ref, k_wide, q_wide, dq_acc):
    k_wide[:, :HD] = kv_ref[0]
    k_wide[:, HD:] = key_hot[...]
    q_wide[:, :HD] = qr_ref[0]
    q_wide[:, HD:] = row_bar[...]
    factor = SCALE * LOG2E

    def stats(chunk, carry):
        top, total, weighted = carry
        rows = rows_of(chunk)
        raw = nt(k_wide[rows, :], q_wide[...])
        dots = nt(kv_ref[1, rows, :], qr_ref[1])
        new_top = jnp.maximum(top, raw.max(axis=0, keepdims=True))
        weights = jnp.exp2((raw - new_top) * factor)
        shrink = jnp.exp2((top - new_top) * factor)
        return (
            new_top,
            total * shrink + weights.sum(axis=0, keepdims=True),
            weighted * shrink + (weights * dots).sum(axis=0, keepdims=True),
        )

    zero = jnp.zeros((1, ROWS), jnp.float32)
    top, total, weighted = lax.fori_loop(
        0, TOKENS // CHUNK, stats, (jnp.full((1, ROWS), BARRED, jnp.float32), zero, zero)
    )
    norm = top * factor + jnp.log2(total)
    row_dots = weighted / total
    norm_ref[...] = norm
    dq_acc[...] = jnp.zeros_like(dq_acc)

    def grads(chunk, carry):
        rows = rows_of(chunk)
        raw = nt(k_wide[rows, :], q_wide[...])
        dots = nt(kv_ref[1, rows, :], qr_ref[1])
        weights = jnp.exp2(raw * factor - norm)
        slopes = (weights * (dots - row_dots)).astype(jnp.bfloat16)
        dkv_ref[0, rows, :] = (SCALE * nn(slopes, qr_ref[0])).astype(jnp.bfloat16)
        dkv_ref[1, rows, :] = nn(weights.astype(jnp.bfloat16), qr_ref[1]).astype(jnp.bfloat16)
        dq_acc[...] += tn(kv_ref[0, rows, :], slopes)
        return carry

    lax.fori_loop(0, TOKENS // CHUNK, grads, 0)
    dq_ref[...] = (SCALE * dq_acc[...]).T.astype(jnp.bfloat16)


def attention_grads(kv, qr, key_hot, row_bar):
    return pl.pallas_call(
        grads_kernel,
        out_shape=(
            jax.ShapeDtypeStruct((2, TOKENS, HD), jnp.bfloat16),
            jax.ShapeDtypeStruct((ROWS, HD), jnp.bfloat16),
            jax.ShapeDtypeStruct((1, ROWS), jnp.float32),
        ),
        in_specs=[VMEM] * 4,
        out_specs=(VMEM, VMEM, VMEM),
        scratch_shapes=[
            pltpu.VMEM((TOKENS, 2 * HD), jnp.bfloat16),
            pltpu.VMEM((ROWS, 2 * HD), jnp.bfloat16),
            pltpu.VMEM((HD, ROWS), jnp.float32),
        ],
        compiler_params=pltpu.CompilerParams(vmem_limit_bytes=48 << 20),
        name="attention_grads",
    )(kv, qr, key_hot, row_bar)


def tangent_kernel(
    kv_ref, q_ref, dot_ref, qdot_ref, key_hot, row_bar, norm_ref, out_ref, k_wide, q_wide, kk_wide, qq_wide, vv_wide, acc, plain
):
    k_wide[:, :HD] = kv_ref[0]
    k_wide[:, HD:] = key_hot[...]
    q_wide[:, :HD] = q_ref[...]
    q_wide[:, HD:] = row_bar[...]
    kk_wide[:, :HD] = kv_ref[0]
    kk_wide[:, HD:] = dot_ref[0]
    qq_wide[:, :HD] = qdot_ref[...]
    qq_wide[:, HD:] = q_ref[...]
    vv_wide[:, :HD] = kv_ref[1]
    vv_wide[:, HD:] = dot_ref[1]
    factor = SCALE * LOG2E
    norm = norm_ref[...]
    acc[...] = jnp.zeros_like(acc)
    plain[...] = jnp.zeros_like(plain)

    def step(chunk, curve):
        rows = rows_of(chunk)
        raw = nt(k_wide[rows, :], q_wide[...])
        moved = nt(kk_wide[rows, :], qq_wide[...])
        weights = jnp.exp2(raw * factor - norm)
        turned = weights * (moved * SCALE)
        acc[...] += tn(kv_ref[1, rows, :], turned.astype(jnp.bfloat16))
        plain[...] += tn(vv_wide[rows, :], weights.astype(jnp.bfloat16))
        return curve + turned.sum(axis=0, keepdims=True)

    curve = lax.fori_loop(0, TOKENS // CHUNK, step, jnp.zeros((1, ROWS), jnp.float32))
    total = acc[...] + plain[HD:, :] - curve * plain[:HD, :]
    out_ref[...] = total.T.astype(jnp.bfloat16)


def attention_tangent(kv, q, dots, qdot, key_hot, row_bar, norm):
    return pl.pallas_call(
        tangent_kernel,
        out_shape=jax.ShapeDtypeStruct((ROWS, HD), jnp.bfloat16),
        in_specs=[VMEM] * 7,
        out_specs=VMEM,
        scratch_shapes=[
            pltpu.VMEM((TOKENS, 2 * HD), jnp.bfloat16),
            pltpu.VMEM((ROWS, 2 * HD), jnp.bfloat16),
            pltpu.VMEM((TOKENS, 2 * HD), jnp.bfloat16),
            pltpu.VMEM((ROWS, 2 * HD), jnp.bfloat16),
            pltpu.VMEM((TOKENS, 2 * HD), jnp.bfloat16),
            pltpu.VMEM((HD, ROWS), jnp.float32),
            pltpu.VMEM((2 * HD, ROWS), jnp.float32),
        ],
        compiler_params=pltpu.CompilerParams(vmem_limit_bytes=48 << 20),
        name="attention_tangent",
    )(kv, q, dots, qdot, key_hot, row_bar, norm)


def mask_sides(token_latent_frame, frame_mask):
    frame_count = frame_mask.shape[0]
    lanes = jnp.arange(HD, dtype=jnp.int32)
    key_hot = (token_latent_frame[:, None] == lanes).astype(jnp.bfloat16)
    chip, core = place()
    first = start_of(chip % 3)
    blocks = token_latent_frame.reshape(CHIPS, 2, HD)
    mine = jnp.minimum(first + jnp.arange(SLOTS, dtype=jnp.int32), CHIPS - 1)
    own_frames = blocks[mine, core].reshape(ROWS)
    barred = jnp.pad(jnp.where(frame_mask == 1, 0.0, 1.0), ((0, 0), (0, HD - frame_count)))
    own_hot = (own_frames[:, None] == jnp.arange(frame_count, dtype=jnp.int32)).astype(jnp.float32)
    row_bar = (jnp.dot(own_hot, barred) * BARRED).astype(jnp.bfloat16)
    return key_hot, row_bar


def by_head(rows):
    return jnp.swapaxes(rows.reshape(rows.shape[:-1] + (HEADS, HD)), -3, -2)


def to_rows(heads):
    swapped = jnp.swapaxes(heads, -3, -2)
    return swapped.reshape(swapped.shape[:-2] + (HEADS * HD,))


def on_device(clip_tokens, w_qkv, readout, token_latent_frame, frame_mask):
    key_hot, row_bar = mask_sides(token_latent_frame, frame_mask)
    tokens_all = lax.all_gather(clip_tokens, "head", axis=0, tiled=True)
    projected = jnp.einsum(
        "td,cde->cte", tokens_all, w_qkv, preferred_element_type=jnp.float32
    ).astype(jnp.bfloat16)
    heads = by_head(projected)
    kv, qr = deal(heads[1:], jnp.stack([heads[0], by_head(readout)]), 0)
    kv = kv.reshape(2, TOKENS, HD)
    qr = qr.reshape(2, ROWS, HD)
    dkv, dq, norm = attention_grads(kv, qr, key_hot, row_bar)
    kv_grad, q_grad = reduce_back(
        dkv.reshape(2, CHIPS, 2, HD, HD), dq.reshape(SLOTS, HD, HD), 1
    )
    grads = to_rows(jnp.concatenate([q_grad[None], kv_grad]))
    partial_input = jnp.einsum("cte,cde->td", grads, w_qkv, preferred_element_type=jnp.float32)
    input_sum = lax.psum(partial_input.astype(jnp.bfloat16), "head")
    panel_rows = clip_tokens.shape[0]
    grad_x = lax.dynamic_slice_in_dim(input_sum, lax.axis_index("head") * panel_rows, panel_rows)
    tangents = jnp.einsum(
        "td,cde->cte", input_sum, w_qkv, preferred_element_type=jnp.float32
    ).astype(jnp.bfloat16)
    dot_heads = by_head(tangents)
    kv_dot, q_dot = deal(dot_heads[1:], dot_heads[:1], 2)
    out = attention_tangent(
        kv, qr[0], kv_dot.reshape(2, TOKENS, HD), q_dot.reshape(ROWS, HD), key_hot, row_bar, norm
    )
    penalty_grad = to_rows(return_queries(out.reshape(SLOTS, HD, HD), 3))
    return (grad_x, penalty_grad)


def solution(mesh):
    return jax.shard_map(
        on_device,
        mesh=mesh,
        in_specs=(P(("seq", "head"), None), P(None, None, "head"), P("seq", "head"), P(), P()),
        out_specs=(P(("seq", "head"), None), P("seq", "head")),
        check_vma=False,
    )
```

```python
import functools
import math

import jax
import jax.numpy as jnp
from jax import lax
from jax.experimental import pallas as pl
from jax.experimental.pallas import tpu as pltpu
from jax.sharding import PartitionSpec as P

HD = 128
MESH = pl.DeviceIdType.MESH
LOG2E = math.log2(math.e)
BARRED = -1e30

CHIPS = 16
BUSY = 15
HEADS = 5
SLOTS = 6


def start_of(third):
    return (CHIPS * third + 2) // 3


def third_of(chip):
    return (chip * 3) // CHIPS


def place():
    me = lax.axis_index("seq")
    return me // 2, me % 2


PANELS = 10
LAYERS = 4


def enter(chip, core, layers=False):
    barrier = pltpu.get_barrier_semaphore()

    def greet(step, carry):
        peer = (chip + step) % CHIPS
        pl.semaphore_signal(barrier, inc=1, device_id={"seq": 2 * peer + core}, device_id_type=MESH)
        return carry

    lax.fori_loop(1, CHIPS, greet, 0)
    pl.semaphore_signal(barrier, inc=1, device_id={"seq": 2 * chip + 1 - core}, device_id_type=MESH)
    if layers:
        layer = lax.axis_index("head")
        for step in (1, LAYERS - 1):
            pl.semaphore_signal(
                barrier, inc=1, device_id={"head": (layer + step) % LAYERS}, device_id_type=MESH
            )
    pl.semaphore_wait(barrier, CHIPS + (2 if layers else 0))


def remote(src, dst, send_sem, recv_sem, device, axis="seq"):
    return pltpu.make_async_remote_copy(
        src_ref=src,
        dst_ref=dst,
        send_sem=send_sem,
        recv_sem=recv_sem,
        device_id={axis: device},
        device_id_type=MESH,
    )


def deal_queries(chip, core, src, dst, send, recv):
    third = third_of(chip)
    slot = chip - start_of(third)
    own_third = chip % 3
    first = start_of(own_third)
    count = start_of(own_third + 1) - first
    partner = 2 * chip + 1 - core

    def copy(h):
        return remote(src.at[h], dst.at[slot], send.at[h], recv.at[slot], 2 * (3 * h + third) + core)

    def own():
        return pltpu.make_async_copy(src.at[chip // 3], dst.at[slot], recv.at[slot])

    def begin():
        def go(h, carry):
            @pl.when(3 * h + third != chip)
            def _():
                copy(h).start()

            @pl.when(3 * h + third == chip)
            def _():
                own().start()

            return carry

        lax.fori_loop(0, HEADS, go, 0)

    def arrived():
        @pl.when(chip < BUSY)
        def _():
            def come(n, carry):
                @pl.when(first + n != chip)
                def _():
                    remote(src.at[0], dst.at[n], send.at[0], recv.at[n], partner).wait_recv()

                @pl.when(first + n == chip)
                def _():
                    own().wait()

                return carry

            lax.fori_loop(0, count, come, 0)

            @pl.when(count < SLOTS)
            def _():
                dst[SLOTS - 1] = jnp.zeros_like(dst[SLOTS - 1])

    def sent():
        def gone(h, carry):
            @pl.when(3 * h + third != chip)
            def _():
                copy(h).wait_send()

            return carry

        lax.fori_loop(0, HEADS, gone, 0)

    return begin, arrived, sent


def deal_keys(chip, core, src, dst, kv_send, kv_recv, pass_send, pass_recv):
    partner = 2 * chip + 1 - core

    def copy(d):
        return remote(src.at[:, d // 3], dst.at[:, chip, core], kv_send.at[d], kv_recv.at[chip], 2 * d + core)

    def own():
        return pltpu.make_async_copy(src.at[:, chip // 3], dst.at[:, chip, core], kv_recv.at[chip])

    def pass_copy(source, half):
        return remote(
            dst.at[:, source, half], dst.at[:, source, half], pass_send.at[source], pass_recv.at[source], partner
        )

    def begin():
        def go(step, carry):
            d = (chip + step) % CHIPS

            @pl.when(jnp.logical_and(d < BUSY, step > 0))
            def _():
                copy(d).start()

            @pl.when(jnp.logical_and(d < BUSY, step == 0))
            def _():
                own().start()

            return carry

        lax.fori_loop(0, CHIPS, go, 0)

    def arrived():
        @pl.when(chip < BUSY)
        def _():
            def come(step, carry):
                source = (chip + CHIPS - step) % CHIPS

                @pl.when(step > 0)
                def _():
                    remote(
                        src.at[:, 0], dst.at[:, source, core], kv_send.at[0], kv_recv.at[source], partner
                    ).wait_recv()

                @pl.when(step == 0)
                def _():
                    own().wait()

                pass_copy(source, core).start()
                return carry

            lax.fori_loop(0, CHIPS, come, 0)

            def passed(step, carry):
                source = (chip + CHIPS - step) % CHIPS
                pass_copy(source, 1 - core).wait_recv()
                pass_copy(source, core).wait_send()
                return carry

            lax.fori_loop(0, CHIPS, passed, 0)

    def sent():
        def gone(step, carry):
            d = (chip + step) % CHIPS

            @pl.when(d < BUSY)
            def _():
                copy(d).wait_send()

            return carry

        lax.fori_loop(1, CHIPS, gone, 0)

    return begin, arrived, sent


VMEM = pl.BlockSpec(memory_space=pltpu.VMEM)
HBM = pl.BlockSpec(memory_space=pl.ANY)
DMA = pltpu.SemaphoreType.DMA


class Gather:
    def __init__(self, rows_ref, own_send, pass_send, recv):
        self.ref, self.own_send, self.pass_send, self.recv = rows_ref, own_send, pass_send, recv
        self.layer = lax.axis_index("head")
        self.right, self.left = (self.layer + 1) % LAYERS, (self.layer + LAYERS - 1) % LAYERS
        self.across = (self.layer + 2) % LAYERS
        self.height = rows_ref.shape[0] // LAYERS
        self.width = rows_ref.shape[1] // PANELS

    def rows(self, layer):
        return pl.ds(pl.multiple_of(layer * self.height, self.height), self.height)

    def columns(self, panel):
        return pl.ds(panel * self.width, self.width)

    def block(self, layer, panel):
        return self.ref.at[self.rows(layer), self.columns(panel)]

    def copy(self, layer, panel, send, kind, target):
        block = self.block(layer, panel)
        return remote(block, block, send, self.recv.at[kind, panel], target, "head")

    def own(self, panel):
        return (
            self.copy(self.layer, panel, self.own_send.at[0, panel], 0, self.right),
            self.copy(self.layer, panel, self.own_send.at[1, panel], 1, self.left),
        )

    def start(self, panel):
        for copy in self.own(panel):
            copy.start()

    def passing(self, panel):
        if panel % 2 == 0:
            return self.copy(self.left, panel, self.pass_send.at[panel], 2, self.right)
        return self.copy(self.right, panel, self.pass_send.at[panel], 2, self.left)

    def relay(self, panel):
        if panel % 2 == 0:
            self.copy(self.left, panel, self.pass_send.at[panel], 0, self.right).wait_recv()
        else:
            self.copy(self.right, panel, self.pass_send.at[panel], 1, self.left).wait_recv()
        self.passing(panel).start()

    def rest(self, panel):
        if panel % 2 == 0:
            self.copy(self.right, panel, self.pass_send.at[panel], 1, self.left).wait_recv()
        else:
            self.copy(self.left, panel, self.pass_send.at[panel], 0, self.right).wait_recv()
        self.copy(self.across, panel, self.pass_send.at[panel], 2, self.right).wait_recv()

    def sent(self):
        for panel in range(PANELS):
            for copy in self.own(panel):
                copy.wait_send()
            self.passing(panel).wait_send()


GATHER_SEMS = [DMA((2, PANELS)), DMA((PANELS,)), DMA((3, PANELS))]
DEAL_SEMS = [DMA((CHIPS,))] * 4
QUERY_SEMS = [DMA((HEADS,)), DMA((SLOTS,))]


def panel_of_w(w_hbm, w_ref, sems, panel):
    depth = w_ref.shape[1] // PANELS
    rows = pl.ds(panel * depth, depth)
    return pltpu.make_async_copy(w_hbm.at[:, rows], w_ref.at[:, rows], sems.at[panel])


def add_panel(totals, rows_ref, w_ref, panel, first):
    depth = w_ref.shape[1] // PANELS
    span = slice(panel * depth, (panel + 1) * depth)
    for c in range(3):
        term = jnp.dot(rows_ref[:, span], w_ref[c, span, :], preferred_element_type=jnp.float32)
        totals[c] = term if first else totals[c] + term


def split_heads(totals, q_heads, kv_heads):
    for h in range(HEADS):
        span = slice(h * HD, (h + 1) * HD)
        q_heads[h] = totals[0, :, span].astype(jnp.bfloat16)
        kv_heads[0, h] = totals[1, :, span].astype(jnp.bfloat16)
        kv_heads[1, h] = totals[2, :, span].astype(jnp.bfloat16)


def project_kernel(
    x_ref, w_hbm, readout_ref, kv_out, q_out, r_out,
    x_all, w_ref, totals, q_heads, kv_heads, r_heads, w_sems, *sems
):
    chip, core = place()
    for panel in range(PANELS):
        panel_of_w(w_hbm, w_ref, w_sems, panel).start()
    gather = Gather(x_all, *sems[:3])
    x_all[gather.rows(gather.layer), :] = x_ref[...]
    for h in range(HEADS):
        r_heads[h] = readout_ref[:, h * HD : (h + 1) * HD]
    enter(chip, core, layers=True)
    ahead = 3
    for panel in range(ahead):
        gather.start(panel)
    r_begin, r_arrived, r_sent = deal_queries(chip, core, r_heads, r_out, *sems[3:5])
    q_begin, q_arrived, q_sent = deal_queries(chip, core, q_heads, q_out, *sems[5:7])
    kv_begin, kv_arrived, kv_sent = deal_keys(chip, core, kv_heads, kv_out, *sems[7:])
    r_begin()

    gather.relay(0)
    for panel in range(PANELS):
        if panel + ahead < PANELS:
            gather.start(panel + ahead)
        if panel + 1 < PANELS:
            gather.relay(panel + 1)
        gather.rest(panel)
        panel_of_w(w_hbm, w_ref, w_sems, panel).wait()
        add_panel(totals, x_all, w_ref, panel, panel == 0)
    split_heads(totals, q_heads, kv_heads)
    kv_begin()
    q_begin()
    kv_arrived()
    q_arrived()
    r_arrived()
    gather.sent()
    kv_sent()
    q_sent()
    r_sent()


def project(x, w, readout, collective_id):
    tokens, width = LAYERS * x.shape[0], x.shape[1]
    block = jax.ShapeDtypeStruct((SLOTS, HD, HD), jnp.bfloat16)
    return pl.pallas_call(
        project_kernel,
        out_shape=(jax.ShapeDtypeStruct((2, CHIPS, 2, HD, HD), jnp.bfloat16), block, block),
        in_specs=[VMEM, HBM, VMEM],
        out_specs=(VMEM, VMEM, VMEM),
        scratch_shapes=[
            pltpu.VMEM((tokens, width), jnp.bfloat16),
            pltpu.VMEM(w.shape, jnp.bfloat16),
            pltpu.VMEM((3, tokens, HEADS * HD), jnp.float32),
            pltpu.VMEM((HEADS, HD, HD), jnp.bfloat16),
            pltpu.VMEM((2, HEADS, HD, HD), jnp.bfloat16),
            pltpu.VMEM((HEADS, HD, HD), jnp.bfloat16),
            DMA((PANELS,)),
        ]
        + GATHER_SEMS
        + QUERY_SEMS
        + QUERY_SEMS
        + DEAL_SEMS,
        compiler_params=pltpu.CompilerParams(
            collective_id=collective_id, has_side_effects=True, vmem_limit_bytes=48 << 20
        ),
        name="project",
    )(x, w, readout)


def input_grad_kernel(
    q_grad, kv_grad, w_hbm, gx_ref, kv_out, q_out,
    x_all, w_ref, totals, q_heads, kv_heads, grads, parts, via, direct, mixed, mix_out,
    w_sems, via_send, via_recv, direct_send, direct_recv, mix_send, mix_recv, *sems
):
    chip, core = place()
    for panel in range(PANELS):
        panel_of_w(w_hbm, w_ref, w_sems, panel).start()
    gather = Gather(x_all, *sems[:3])
    for h in range(HEADS):
        span = slice(h * HD, (h + 1) * HD)
        grads[0, :, span] = q_grad[h]
        grads[1, :, span] = kv_grad[0, h]
        grads[2, :, span] = kv_grad[1, h]
    enter(chip, core, layers=True)
    q_begin, q_arrived, q_sent = deal_queries(chip, core, q_heads, q_out, *sems[3:5])
    kv_begin, kv_arrived, kv_sent = deal_keys(chip, core, kv_heads, kv_out, *sems[5:])
    depth = gather.width

    def near_far(panel):
        return (gather.right, gather.left) if panel % 2 == 0 else (gather.left, gather.right)

    def part(layer, panel):
        return parts.at[gather.rows(layer), gather.columns(panel)]

    def piece(ref, panel):
        return ref.at[:, gather.columns(panel)]

    def via_copy(panel):
        return remote(
            part(gather.across, panel), piece(via, panel), via_send.at[panel], via_recv.at[panel],
            near_far(panel)[1], "head",
        )

    def direct_copy(panel):
        target = near_far(panel)[0]
        return remote(
            part(target, panel), piece(direct, panel), direct_send.at[panel], direct_recv.at[panel], target, "head"
        )

    def mix_copy(panel):
        return remote(
            piece(mix_out, panel), piece(mixed, panel), mix_send.at[panel], mix_recv.at[panel],
            near_far(panel)[1], "head",
        )

    def share(panel):
        span = slice(panel * depth, (panel + 1) * depth)
        panel_of_w(w_hbm, w_ref, w_sems, panel).wait()
        total = nt(grads[0], w_ref[0, span, :])
        total += nt(grads[1], w_ref[1, span, :])
        total += nt(grads[2], w_ref[2, span, :])
        parts[:, span] = total.astype(jnp.bfloat16)
        via_copy(panel).start()
        direct_copy(panel).start()

    def mix(panel):
        span = slice(panel * depth, (panel + 1) * depth)
        via_copy(panel).wait_recv()
        mine = parts[gather.rows(near_far(panel)[1]), span]
        mix_out[:, span] = (via[:, span].astype(jnp.float32) + mine.astype(jnp.float32)).astype(jnp.bfloat16)
        mix_copy(panel).start()

    def settle(panel):
        span = slice(panel * depth, (panel + 1) * depth)
        direct_copy(panel).wait_recv()
        mix_copy(panel).wait_recv()
        mine = parts[gather.rows(gather.layer), span].astype(jnp.float32)
        total = mine + direct[:, span].astype(jnp.float32) + mixed[:, span].astype(jnp.float32)
        total = total.astype(jnp.bfloat16)
        gx_ref[:, span] = total
        x_all[gather.rows(gather.layer), span] = total
        gather.start(panel)

    def absorb(panel):
        gather.rest(panel)
        add_panel(totals, x_all, w_ref, panel, panel == 0)

    stages = ((share, 0), (mix, 1), (settle, 3), (gather.relay, 4), (absorb, 6))
    for step in range(PANELS + 6):
        for stage, lag in stages:
            if 0 <= step - lag < PANELS:
                stage(step - lag)
    split_heads(totals, q_heads, kv_heads)
    kv_begin()
    q_begin()
    kv_arrived()
    q_arrived()
    gather.sent()
    for panel in range(PANELS):
        via_copy(panel).wait_send()
        direct_copy(panel).wait_send()
        mix_copy(panel).wait_send()
    kv_sent()
    q_sent()


def input_grad(q_grad, kv_grad, w, collective_id):
    tokens, width = HD, w.shape[1]
    rows = tokens // LAYERS
    return pl.pallas_call(
        input_grad_kernel,
        out_shape=(
            jax.ShapeDtypeStruct((rows, width), jnp.bfloat16),
            jax.ShapeDtypeStruct((2, CHIPS, 2, HD, HD), jnp.bfloat16),
            jax.ShapeDtypeStruct((SLOTS, HD, HD), jnp.bfloat16),
        ),
        in_specs=[VMEM, VMEM, HBM],
        out_specs=(VMEM, VMEM, VMEM),
        scratch_shapes=[
            pltpu.VMEM((tokens, width), jnp.bfloat16),
            pltpu.VMEM(w.shape, jnp.bfloat16),
            pltpu.VMEM((3, tokens, HEADS * HD), jnp.float32),
            pltpu.VMEM((HEADS, HD, HD), jnp.bfloat16),
            pltpu.VMEM((2, HEADS, HD, HD), jnp.bfloat16),
            pltpu.VMEM((3, tokens, HEADS * HD), jnp.bfloat16),
            pltpu.VMEM((tokens, width), jnp.bfloat16),
        ]
        + [pltpu.VMEM((rows, width), jnp.bfloat16)] * 4
        + [DMA((PANELS,))] * 7
        + GATHER_SEMS
        + QUERY_SEMS
        + DEAL_SEMS,
        compiler_params=pltpu.CompilerParams(
            collective_id=collective_id, has_side_effects=True, vmem_limit_bytes=48 << 20
        ),
        name="input_grad",
    )(q_grad, kv_grad, w)


def give_back(chip, core, src, dst, send, recv):
    own_third = chip % 3
    first = start_of(own_third)
    count = start_of(own_third + 1) - first
    third = third_of(chip)
    own_head = chip // 3

    def out_copy(n):
        return remote(src.at[n], dst.at[own_head], send.at[n], recv.at[own_head], 2 * (first + n) + core)

    def own():
        return pltpu.make_async_copy(src.at[chip - first], dst.at[own_head], recv.at[own_head])

    def begin():
        @pl.when(chip < BUSY)
        def _():
            def go(n, carry):
                @pl.when(first + n != chip)
                def _():
                    out_copy(n).start()

                @pl.when(first + n == chip)
                def _():
                    own().start()

                return carry

            lax.fori_loop(0, count, go, 0)

    def end():
        def come(h, carry):
            @pl.when(3 * h + third != chip)
            def _():
                remote(src.at[0], dst.at[h], send.at[0], recv.at[h], 2 * chip + 1 - core).wait_recv()

            @pl.when(3 * h + third == chip)
            def _():
                own().wait()

            return carry

        lax.fori_loop(0, HEADS, come, 0)

        @pl.when(chip < BUSY)
        def _():
            def gone(n, carry):
                @pl.when(first + n != chip)
                def _():
                    out_copy(n).wait_send()

                return carry

            lax.fori_loop(0, count, gone, 0)

    return begin, end


def return_kernel(dq_ref, q_out, q_send, q_recv):
    chip, core = place()
    enter(chip, core)
    begin, end = give_back(chip, core, dq_ref, q_out, q_send, q_recv)
    begin()
    end()


def return_queries(dq, collective_id):
    return pl.pallas_call(
        return_kernel,
        out_shape=jax.ShapeDtypeStruct((HEADS, HD, HD), jnp.bfloat16),
        in_specs=[VMEM],
        out_specs=VMEM,
        scratch_shapes=[DMA((SLOTS,)), DMA((HEADS,))],
        compiler_params=pltpu.CompilerParams(
            collective_id=collective_id, has_side_effects=True, vmem_limit_bytes=32 << 20
        ),
        name="return_queries",
    )(dq)


def reduce_kernel(
    dkv_ref, dq_ref, kv_sum, q_out, other, mixed, landed, x_send, x_recv, kv_send, kv_recv, q_send, q_recv
):
    chip, core = place()
    partner = 2 * chip + 1 - core
    enter(chip, core)
    begin, end = give_back(chip, core, dq_ref, q_out, q_send, q_recv)

    def swap(target):
        return remote(
            dkv_ref.at[:, target, 1 - core], other.at[:, target], x_send.at[target], x_recv.at[target], partner
        )

    def out_copy(target):
        return remote(
            mixed.at[:, target], landed.at[chip], kv_send.at[target], kv_recv.at[chip], 2 * target + core
        )

    def own():
        return pltpu.make_async_copy(mixed.at[:, chip], landed.at[chip], kv_recv.at[chip])

    @pl.when(chip < BUSY)
    def _():
        def start_swap(step, carry):
            swap((chip + step) % CHIPS).start()
            return carry

        lax.fori_loop(0, CHIPS, start_swap, 0)

    begin()

    @pl.when(chip < BUSY)
    def _():
        def mix(step, carry):
            target = (chip + step) % CHIPS
            swap(target).wait_recv()
            mixed[:, target] = (
                dkv_ref[:, target, core].astype(jnp.float32) + other[:, target].astype(jnp.float32)
            ).astype(jnp.bfloat16)

            @pl.when(step > 0)
            def _():
                out_copy(target).start()

            @pl.when(step == 0)
            def _():
                own().start()

            return carry

        lax.fori_loop(0, CHIPS, mix, 0)

    def come(step, carry):
        source = (chip + CHIPS - step) % CHIPS

        @pl.when(jnp.logical_and(source < BUSY, step > 0))
        def _():
            remote(
                mixed.at[:, 0], landed.at[source], kv_send.at[0], kv_recv.at[source], partner
            ).wait_recv()

        @pl.when(jnp.logical_and(source < BUSY, step == 0))
        def _():
            own().wait()

        return carry

    lax.fori_loop(0, CHIPS, come, 0)

    def add_up(h, carry):
        total = landed[3 * h].astype(jnp.float32) + landed[3 * h + 1].astype(jnp.float32)
        kv_sum[:, h] = (total + landed[3 * h + 2].astype(jnp.float32)).astype(jnp.bfloat16)
        return carry

    lax.fori_loop(0, HEADS, add_up, 0)
    end()

    @pl.when(chip < BUSY)
    def _():
        def gone(step, carry):
            target = (chip + step) % CHIPS
            swap(target).wait_send()

            @pl.when(step > 0)
            def _():
                out_copy(target).wait_send()

            return carry

        lax.fori_loop(0, CHIPS, gone, 0)


def reduce_back(dkv, dq, collective_id):
    return pl.pallas_call(
        reduce_kernel,
        out_shape=(
            jax.ShapeDtypeStruct((2, HEADS, HD, HD), jnp.bfloat16),
            jax.ShapeDtypeStruct((HEADS, HD, HD), jnp.bfloat16),
        ),
        in_specs=[VMEM] * 2,
        out_specs=(VMEM, VMEM),
        scratch_shapes=[
            pltpu.VMEM((2, CHIPS, HD, HD), jnp.bfloat16),
            pltpu.VMEM((2, CHIPS, HD, HD), jnp.bfloat16),
            pltpu.VMEM((CHIPS, 2, HD, HD), jnp.bfloat16),
            DMA((CHIPS,)),
            DMA((CHIPS,)),
            DMA((CHIPS,)),
            DMA((CHIPS,)),
            DMA((SLOTS,)),
            DMA((HEADS,)),
        ],
        compiler_params=pltpu.CompilerParams(
            collective_id=collective_id, has_side_effects=True, vmem_limit_bytes=32 << 20
        ),
        name="reduce_back",
    )(dkv, dq)


TOKENS = 4096
ROWS = SLOTS * HD
CHUNK = 256
SCALE = HD ** (-0.5)


def nt(left, right):
    return lax.dot_general(left, right, (((1,), (1,)), ((), ())), preferred_element_type=jnp.float32)


def nn(left, right):
    return lax.dot_general(left, right, (((1,), (0,)), ((), ())), preferred_element_type=jnp.float32)


def tn(left, right):
    return lax.dot_general(left, right, (((0,), (0,)), ((), ())), preferred_element_type=jnp.float32)


def rows_of(chunk):
    return pl.ds(pl.multiple_of(chunk * CHUNK, CHUNK), CHUNK)


def grads_kernel(kv_ref, q_ref, r_ref, key_hot, row_bar, dkv_ref, dq_ref, norm_ref, k_wide, q_wide, dq_acc):
    k_wide[:, :HD] = kv_ref[0]
    k_wide[:, HD:] = key_hot[...]
    q_wide[:, :HD] = q_ref[...]
    q_wide[:, HD:] = row_bar[...]
    factor = SCALE * LOG2E

    def stats(chunk, carry):
        top, total, weighted = carry
        rows = rows_of(chunk)
        raw = nt(k_wide[rows, :], q_wide[...])
        dots = nt(kv_ref[1, rows, :], r_ref[...])
        new_top = jnp.maximum(top, raw.max(axis=0, keepdims=True))
        weights = jnp.exp2((raw - new_top) * factor)
        shrink = jnp.exp2((top - new_top) * factor)
        return (
            new_top,
            total * shrink + weights.sum(axis=0, keepdims=True),
            weighted * shrink + (weights * dots).sum(axis=0, keepdims=True),
        )

    zero = jnp.zeros((1, ROWS), jnp.float32)
    top, total, weighted = lax.fori_loop(
        0, TOKENS // CHUNK, stats, (jnp.full((1, ROWS), BARRED, jnp.float32), zero, zero)
    )
    norm = top * factor + jnp.log2(total)
    row_dots = weighted / total
    norm_ref[...] = norm
    dq_acc[...] = jnp.zeros_like(dq_acc)

    def grads(chunk, carry):
        rows = rows_of(chunk)
        raw = nt(k_wide[rows, :], q_wide[...])
        dots = nt(kv_ref[1, rows, :], r_ref[...])
        weights = jnp.exp2(raw * factor - norm)
        slopes = (weights * (dots - row_dots)).astype(jnp.bfloat16)
        dkv_ref[0, rows, :] = (SCALE * nn(slopes, q_ref[...])).astype(jnp.bfloat16)
        dkv_ref[1, rows, :] = nn(weights.astype(jnp.bfloat16), r_ref[...]).astype(jnp.bfloat16)
        dq_acc[...] += tn(kv_ref[0, rows, :], slopes)
        return carry

    lax.fori_loop(0, TOKENS // CHUNK, grads, 0)
    dq_ref[...] = (SCALE * dq_acc[...]).T.astype(jnp.bfloat16)


def attention_grads(kv, q, r, key_hot, row_bar):
    return pl.pallas_call(
        grads_kernel,
        out_shape=(
            jax.ShapeDtypeStruct((2, TOKENS, HD), jnp.bfloat16),
            jax.ShapeDtypeStruct((ROWS, HD), jnp.bfloat16),
            jax.ShapeDtypeStruct((1, ROWS), jnp.float32),
        ),
        in_specs=[VMEM] * 5,
        out_specs=(VMEM, VMEM, VMEM),
        scratch_shapes=[
            pltpu.VMEM((TOKENS, 2 * HD), jnp.bfloat16),
            pltpu.VMEM((ROWS, 2 * HD), jnp.bfloat16),
            pltpu.VMEM((HD, ROWS), jnp.float32),
        ],
        compiler_params=pltpu.CompilerParams(vmem_limit_bytes=48 << 20),
        name="attention_grads",
    )(kv, q, r, key_hot, row_bar)


def tangent_kernel(
    kv_ref, q_ref, dot_ref, qdot_ref, key_hot, row_bar, norm_ref, out_ref, k_wide, q_wide, kk_wide, qq_wide, vv_wide, acc, plain
):
    k_wide[:, :HD] = kv_ref[0]
    k_wide[:, HD:] = key_hot[...]
    q_wide[:, :HD] = q_ref[...]
    q_wide[:, HD:] = row_bar[...]
    kk_wide[:, :HD] = kv_ref[0]
    kk_wide[:, HD:] = dot_ref[0]
    qq_wide[:, :HD] = qdot_ref[...]
    qq_wide[:, HD:] = q_ref[...]
    vv_wide[:, :HD] = kv_ref[1]
    vv_wide[:, HD:] = dot_ref[1]
    factor = SCALE * LOG2E
    norm = norm_ref[...]
    acc[...] = jnp.zeros_like(acc)
    plain[...] = jnp.zeros_like(plain)

    def step(chunk, curve):
        rows = rows_of(chunk)
        raw = nt(k_wide[rows, :], q_wide[...])
        moved = nt(kk_wide[rows, :], qq_wide[...])
        weights = jnp.exp2(raw * factor - norm)
        turned = weights * (moved * SCALE)
        acc[...] += tn(kv_ref[1, rows, :], turned.astype(jnp.bfloat16))
        plain[...] += tn(vv_wide[rows, :], weights.astype(jnp.bfloat16))
        return curve + turned.sum(axis=0, keepdims=True)

    curve = lax.fori_loop(0, TOKENS // CHUNK, step, jnp.zeros((1, ROWS), jnp.float32))
    total = acc[...] + plain[HD:, :] - curve * plain[:HD, :]
    out_ref[...] = total.T.astype(jnp.bfloat16)


def attention_tangent(kv, q, dots, qdot, key_hot, row_bar, norm):
    return pl.pallas_call(
        tangent_kernel,
        out_shape=jax.ShapeDtypeStruct((ROWS, HD), jnp.bfloat16),
        in_specs=[VMEM] * 7,
        out_specs=VMEM,
        scratch_shapes=[
            pltpu.VMEM((TOKENS, 2 * HD), jnp.bfloat16),
            pltpu.VMEM((ROWS, 2 * HD), jnp.bfloat16),
            pltpu.VMEM((TOKENS, 2 * HD), jnp.bfloat16),
            pltpu.VMEM((ROWS, 2 * HD), jnp.bfloat16),
            pltpu.VMEM((TOKENS, 2 * HD), jnp.bfloat16),
            pltpu.VMEM((HD, ROWS), jnp.float32),
            pltpu.VMEM((2 * HD, ROWS), jnp.float32),
        ],
        compiler_params=pltpu.CompilerParams(vmem_limit_bytes=48 << 20),
        name="attention_tangent",
    )(kv, q, dots, qdot, key_hot, row_bar, norm)


def mask_sides(token_latent_frame, frame_mask):
    frame_count = frame_mask.shape[0]
    lanes = jnp.arange(HD, dtype=jnp.int32)
    key_hot = (token_latent_frame[:, None] == lanes).astype(jnp.bfloat16)
    chip, core = place()
    first = start_of(chip % 3)
    blocks = token_latent_frame.reshape(CHIPS, 2, HD)
    mine = jnp.minimum(first + jnp.arange(SLOTS, dtype=jnp.int32), CHIPS - 1)
    own_frames = blocks[mine, core].reshape(ROWS)
    barred = jnp.pad(jnp.where(frame_mask == 1, 0.0, 1.0), ((0, 0), (0, HD - frame_count)))
    own_hot = (own_frames[:, None] == jnp.arange(frame_count, dtype=jnp.int32)).astype(jnp.float32)
    row_bar = (jnp.dot(own_hot, barred) * BARRED).astype(jnp.bfloat16)
    return key_hot, row_bar


def to_rows(heads):
    swapped = jnp.swapaxes(heads, -3, -2)
    return swapped.reshape(swapped.shape[:-2] + (HEADS * HD,))


def on_device(clip_tokens, w_qkv, readout, token_latent_frame, frame_mask):
    key_hot, row_bar = mask_sides(token_latent_frame, frame_mask)
    kv, q, r = project(clip_tokens, w_qkv, readout, 0)
    kv = kv.reshape(2, TOKENS, HD)
    q = q.reshape(ROWS, HD)
    dkv, dq, norm = attention_grads(kv, q, r.reshape(ROWS, HD), key_hot, row_bar)
    kv_grad, q_grad = reduce_back(
        dkv.reshape(2, CHIPS, 2, HD, HD), dq.reshape(SLOTS, HD, HD), 1
    )
    grad_x, kv_dot, q_dot = input_grad(q_grad, kv_grad, w_qkv, 2)
    out = attention_tangent(
        kv, q, kv_dot.reshape(2, TOKENS, HD), q_dot.reshape(ROWS, HD), key_hot, row_bar, norm
    )
    penalty_grad = to_rows(return_queries(out.reshape(SLOTS, HD, HD), 3))
    return (grad_x, penalty_grad)


def solution(mesh):
    return jax.shard_map(
        on_device,
        mesh=mesh,
        in_specs=(P(("seq", "head"), None), P(None, None, "head"), P("seq", "head"), P(), P()),
        out_specs=(P(("seq", "head"), None), P("seq", "head")),
        check_vma=False,
    )
```

```python
import functools
import math

import jax
import jax.numpy as jnp
from jax import lax
from jax.experimental import pallas as pl
from jax.experimental.pallas import tpu as pltpu
from jax.sharding import PartitionSpec as P

HD = 128
MESH = pl.DeviceIdType.MESH
LOG2E = math.log2(math.e)
BARRED = -1e30

CHIPS = 16
BUSY = 15
HEADS = 5
SLOTS = 6
LAG = 2


def start_of(third):
    return (CHIPS * third + 2) // 3


def third_of(chip):
    return (chip * 3) // CHIPS


def place():
    me = lax.axis_index("seq")
    return me // 2, me % 2


PANELS = 10
LAYERS = 4


def enter(chip, core, layers=False):
    barrier = pltpu.get_barrier_semaphore()

    def greet(step, carry):
        peer = (chip + step) % CHIPS
        pl.semaphore_signal(barrier, inc=1, device_id={"seq": 2 * peer + core}, device_id_type=MESH)
        return carry

    lax.fori_loop(1, CHIPS, greet, 0)
    pl.semaphore_signal(barrier, inc=1, device_id={"seq": 2 * chip + 1 - core}, device_id_type=MESH)
    if layers:
        layer = lax.axis_index("head")
        for step in (1, LAYERS - 1):
            pl.semaphore_signal(
                barrier, inc=1, device_id={"head": (layer + step) % LAYERS}, device_id_type=MESH
            )
    pl.semaphore_wait(barrier, CHIPS + (2 if layers else 0))


def remote(src, dst, send_sem, recv_sem, device, axis="seq"):
    return pltpu.make_async_remote_copy(
        src_ref=src,
        dst_ref=dst,
        send_sem=send_sem,
        recv_sem=recv_sem,
        device_id={axis: device},
        device_id_type=MESH,
    )


def deal_queries(chip, core, src, dst, send, recv):
    third = third_of(chip)
    slot = chip - start_of(third)
    own_third = chip % 3
    first = start_of(own_third)
    count = start_of(own_third + 1) - first
    partner = 2 * chip + 1 - core

    def copy(h):
        return remote(src.at[h], dst.at[slot], send.at[h], recv.at[slot], 2 * (3 * h + third) + core)

    def own():
        return pltpu.make_async_copy(src.at[chip // 3], dst.at[slot], recv.at[slot])

    def begin():
        def go(h, carry):
            @pl.when(3 * h + third != chip)
            def _():
                copy(h).start()

            @pl.when(3 * h + third == chip)
            def _():
                own().start()

            return carry

        lax.fori_loop(0, HEADS, go, 0)

    def arrived():
        @pl.when(chip < BUSY)
        def _():
            def come(n, carry):
                @pl.when(first + n != chip)
                def _():
                    remote(src.at[0], dst.at[n], send.at[0], recv.at[n], partner).wait_recv()

                @pl.when(first + n == chip)
                def _():
                    own().wait()

                return carry

            lax.fori_loop(0, count, come, 0)

            @pl.when(count < SLOTS)
            def _():
                dst[SLOTS - 1] = jnp.zeros_like(dst[SLOTS - 1])

    def sent():
        def gone(h, carry):
            @pl.when(3 * h + third != chip)
            def _():
                copy(h).wait_send()

            return carry

        lax.fori_loop(0, HEADS, gone, 0)

    return begin, arrived, sent


def deal_keys(chip, core, src, dst, kv_send, kv_recv, pass_send, pass_recv):
    partner = 2 * chip + 1 - core

    def copy(d):
        return remote(src.at[:, d // 3], dst.at[:, chip, core], kv_send.at[d], kv_recv.at[chip], 2 * d + core)

    def own():
        return pltpu.make_async_copy(src.at[:, chip // 3], dst.at[:, chip, core], kv_recv.at[chip])

    def pass_copy(source, half):
        return remote(
            dst.at[:, source, half], dst.at[:, source, half], pass_send.at[source], pass_recv.at[source], partner
        )

    def begin():
        def go(step, carry):
            d = (chip + step) % CHIPS

            @pl.when(jnp.logical_and(d < BUSY, step > 0))
            def _():
                copy(d).start()

            @pl.when(jnp.logical_and(d < BUSY, step == 0))
            def _():
                own().start()

            return carry

        lax.fori_loop(0, CHIPS, go, 0)

    def source_of(step):
        return (chip + CHIPS - step) % CHIPS

    def arrive(step):
        source = source_of(step)

        @pl.when(step > 0)
        def _():
            remote(
                src.at[:, 0], dst.at[:, source, core], kv_send.at[0], kv_recv.at[source], partner
            ).wait_recv()

        @pl.when(step == 0)
        def _():
            own().wait()

        pass_copy(source, core).start()

    def use(step, body):
        source = source_of(step)
        pass_copy(source, 1 - core).wait_recv()
        body(source)

    def consume(body):
        @pl.when(chip < BUSY)
        def _():
            def first(step, carry):
                arrive(step)
                return carry

            def both(step, carry):
                arrive(step)
                use(step - LAG, body)
                return carry

            def last(step, carry):
                use(step, body)
                return carry

            lax.fori_loop(0, LAG, first, 0)
            lax.fori_loop(LAG, CHIPS, both, 0)
            lax.fori_loop(CHIPS - LAG, CHIPS, last, 0)

    def sent():
        @pl.when(chip < BUSY)
        def _():
            def passed(step, carry):
                pass_copy(source_of(step), core).wait_send()
                return carry

            lax.fori_loop(0, CHIPS, passed, 0)

        def gone(step, carry):
            d = (chip + step) % CHIPS

            @pl.when(d < BUSY)
            def _():
                copy(d).wait_send()

            return carry

        lax.fori_loop(1, CHIPS, gone, 0)

    return begin, consume, sent


VMEM = pl.BlockSpec(memory_space=pltpu.VMEM)
HBM = pl.BlockSpec(memory_space=pl.ANY)
DMA = pltpu.SemaphoreType.DMA


class Gather:
    def __init__(self, rows_ref, own_send, pass_send, recv):
        self.ref, self.own_send, self.pass_send, self.recv = rows_ref, own_send, pass_send, recv
        self.layer = lax.axis_index("head")
        self.right, self.left = (self.layer + 1) % LAYERS, (self.layer + LAYERS - 1) % LAYERS
        self.across = (self.layer + 2) % LAYERS
        self.height = rows_ref.shape[0] // LAYERS
        self.width = rows_ref.shape[1] // PANELS

    def rows(self, layer):
        return pl.ds(pl.multiple_of(layer * self.height, self.height), self.height)

    def columns(self, panel):
        return pl.ds(panel * self.width, self.width)

    def block(self, layer, panel):
        return self.ref.at[self.rows(layer), self.columns(panel)]

    def copy(self, layer, panel, send, kind, target):
        block = self.block(layer, panel)
        return remote(block, block, send, self.recv.at[kind, panel], target, "head")

    def own(self, panel):
        return (
            self.copy(self.layer, panel, self.own_send.at[0, panel], 0, self.right),
            self.copy(self.layer, panel, self.own_send.at[1, panel], 1, self.left),
        )

    def start(self, panel):
        for copy in self.own(panel):
            copy.start()

    def passing(self, panel):
        if panel % 2 == 0:
            return self.copy(self.left, panel, self.pass_send.at[panel], 2, self.right)
        return self.copy(self.right, panel, self.pass_send.at[panel], 2, self.left)

    def relay(self, panel):
        if panel % 2 == 0:
            self.copy(self.left, panel, self.pass_send.at[panel], 0, self.right).wait_recv()
        else:
            self.copy(self.right, panel, self.pass_send.at[panel], 1, self.left).wait_recv()
        self.passing(panel).start()

    def rest(self, panel):
        if panel % 2 == 0:
            self.copy(self.right, panel, self.pass_send.at[panel], 1, self.left).wait_recv()
        else:
            self.copy(self.left, panel, self.pass_send.at[panel], 0, self.right).wait_recv()
        self.copy(self.across, panel, self.pass_send.at[panel], 2, self.right).wait_recv()

    def sent(self):
        for panel in range(PANELS):
            for copy in self.own(panel):
                copy.wait_send()
            self.passing(panel).wait_send()


def panel_of_w(w_hbm, w_ref, sems, panel):
    depth = w_ref.shape[1] // PANELS
    rows = pl.ds(panel * depth, depth)
    return pltpu.make_async_copy(w_hbm.at[:, rows], w_ref.at[:, rows], sems.at[panel])


def add_panel(totals, rows_ref, w_ref, panel, first):
    depth = w_ref.shape[1] // PANELS
    span = slice(panel * depth, (panel + 1) * depth)
    for c in range(3):
        term = jnp.dot(rows_ref[:, span], w_ref[c, span, :], preferred_element_type=jnp.float32)
        totals[c] = term if first else totals[c] + term


def split_heads(totals, q_heads, kv_heads):
    for h in range(HEADS):
        span = slice(h * HD, (h + 1) * HD)
        q_heads[h] = totals[0, :, span].astype(jnp.bfloat16)
        kv_heads[0, h] = totals[1, :, span].astype(jnp.bfloat16)
        kv_heads[1, h] = totals[2, :, span].astype(jnp.bfloat16)


def give_back(chip, core, src, dst, send, recv):
    own_third = chip % 3
    first = start_of(own_third)
    count = start_of(own_third + 1) - first
    third = third_of(chip)
    own_head = chip // 3

    def out_copy(n):
        return remote(src.at[n], dst.at[own_head], send.at[n], recv.at[own_head], 2 * (first + n) + core)

    def own():
        return pltpu.make_async_copy(src.at[chip - first], dst.at[own_head], recv.at[own_head])

    def begin():
        @pl.when(chip < BUSY)
        def _():
            def go(n, carry):
                @pl.when(first + n != chip)
                def _():
                    out_copy(n).start()

                @pl.when(first + n == chip)
                def _():
                    own().start()

                return carry

            lax.fori_loop(0, count, go, 0)

    def end():
        def come(h, carry):
            @pl.when(3 * h + third != chip)
            def _():
                remote(src.at[0], dst.at[h], send.at[0], recv.at[h], 2 * chip + 1 - core).wait_recv()

            @pl.when(3 * h + third == chip)
            def _():
                own().wait()

            return carry

        lax.fori_loop(0, HEADS, come, 0)

        @pl.when(chip < BUSY)
        def _():
            def gone(n, carry):
                @pl.when(first + n != chip)
                def _():
                    out_copy(n).wait_send()

                return carry

            lax.fori_loop(0, count, gone, 0)

    return begin, end


TOKENS = 4096
ROWS = SLOTS * HD
CHUNK = 2 * HD
SCALE = HD ** (-0.5)
FACTOR = SCALE * LOG2E


def nt(left, right):
    return lax.dot_general(left, right, (((1,), (1,)), ((), ())), preferred_element_type=jnp.float32)


def nn(left, right):
    return lax.dot_general(left, right, (((1,), (0,)), ((), ())), preferred_element_type=jnp.float32)


def tn(left, right):
    return lax.dot_general(left, right, (((0,), (0,)), ((), ())), preferred_element_type=jnp.float32)


def mask_sides(frames_ref, mask_ref, key_hot, row_bar, barred, first, core):
    frames = frames_ref[...]
    count = mask_ref.shape[0]
    lane = lax.broadcasted_iota(jnp.int32, (1, HD), 1)
    start = jnp.full((1, HD), TOKENS, jnp.int32)
    end = jnp.full((1, HD), TOKENS, jnp.int32)
    for f in range(count):
        below = jnp.sum((frames < f).astype(jnp.float32), keepdims=True).astype(jnp.int32)
        start = jnp.where(lane == f, below, start)
        end = jnp.where(lane == f - 1, below, end)

    def hot(tokens):
        return jnp.where(jnp.logical_and(tokens >= start, tokens < end), 1.0, 0.0).astype(jnp.bfloat16)

    row = lax.broadcasted_iota(jnp.int32, (HD, HD), 0)

    def fill(block, carry):
        key_hot[pl.ds(pl.multiple_of(block * HD, HD), HD), :] = hot(row + block * HD)
        return carry

    lax.fori_loop(0, TOKENS // HD, fill, 0)
    barred[...] = jnp.zeros_like(barred)
    barred[:count, :count] = jnp.where(mask_ref[...] == 1, 0.0, BARRED)
    table = barred[...].astype(jnp.bfloat16)
    for n in range(SLOTS):
        own = hot(row + (2 * (first + n) + core) * HD)
        row_bar[n * HD : (n + 1) * HD, :] = nn(own, table).astype(jnp.bfloat16)


TOP, TOTAL, WEIGHTED, NORM, ROW_DOTS, CURVE = range(6)


def whole_kernel(
    x_ref, w_hbm, readout_ref, frames_ref, mask_ref, gx_ref, pen_ref,
    w_ref, x_all, gx_all, totals, q_heads, kv_heads, r_heads, qd_heads, kvd_heads,
    kv, dots, q, r, qd, key_hot, row_bar, barred, stat,
    dkv, dq_acc, dq, penalty, other, summed, landed, q_landed, p_landed, plain, grads,
    parts, via, direct, mixed, mix_out,
    w_sems, *sems
):
    sems = list(sems)

    def take(n):
        taken = sems[:n]
        del sems[:n]
        return taken

    chip, core = place()
    partner = 2 * chip + 1 - core
    busy = chip < BUSY
    first = start_of(chip % 3)
    for panel in range(PANELS):
        panel_of_w(w_hbm, w_ref, w_sems, panel).start()
    gather = Gather(x_all, *take(3))
    x_all[gather.rows(gather.layer), :] = x_ref[...]
    for h in range(HEADS):
        r_heads[h] = readout_ref[:, h * HD : (h + 1) * HD]
    enter(chip, core, layers=True)
    ahead = 3
    for panel in range(ahead):
        gather.start(panel)
    r_begin, r_arrived, r_sent = deal_queries(chip, core, r_heads, r, *take(2))
    q_begin, q_arrived, q_sent = deal_queries(chip, core, q_heads, q, *take(2))
    kv_begin, kv_consume, kv_sent = deal_keys(chip, core, kv_heads, kv, *take(4))
    r_begin()
    mask_sides(frames_ref, mask_ref, key_hot, row_bar, barred, first, core)

    gather.relay(0)
    for panel in range(PANELS):
        if panel + ahead < PANELS:
            gather.start(panel + ahead)
        if panel + 1 < PANELS:
            gather.relay(panel + 1)
        gather.rest(panel)
        panel_of_w(w_hbm, w_ref, w_sems, panel).wait()
        add_panel(totals, x_all, w_ref, panel, panel == 0)
    split_heads(totals, q_heads, kv_heads)
    q_begin()
    kv_begin()

    def keys_of(array, source):
        return array[source].reshape(CHUNK, HD)

    def flat(array):
        return array[...].reshape(ROWS, HD)

    def logits(source):
        hot = key_hot[pl.ds(pl.multiple_of(source * CHUNK, CHUNK), CHUNK), :]
        return nt(
            jnp.concatenate([keys_of(kv.at[0], source), hot], axis=1),
            jnp.concatenate([flat(q), row_bar[...]], axis=1),
        )

    def stats(source):
        raw = logits(source)
        readout_dots = nt(keys_of(kv.at[1], source), flat(r))
        top = stat[TOP]
        new_top = jnp.maximum(top, raw.max(axis=0, keepdims=True))
        weights = jnp.exp2((raw - new_top) * FACTOR)
        shrink = jnp.exp2((top - new_top) * FACTOR)
        stat[TOP] = new_top
        stat[TOTAL] = stat[TOTAL] * shrink + weights.sum(axis=0, keepdims=True)
        stat[WEIGHTED] = stat[WEIGHTED] * shrink + (weights * readout_dots).sum(axis=0, keepdims=True)

    q_arrived()
    r_arrived()

    @pl.when(busy)
    def _():
        stat[...] = jnp.zeros_like(stat)
        stat[TOP] = jnp.full((1, ROWS), BARRED, jnp.float32)
        dq_acc[...] = jnp.zeros_like(dq_acc)

    kv_consume(stats)

    def swap(target):
        x_send, x_recv = swap_sems
        return remote(
            dkv.at[:, target, 1 - core], other.at[:, target], x_send.at[target], x_recv.at[target], partner
        )

    def out_copy(target):
        return remote(
            summed.at[:, target], landed.at[chip], sum_sems[0].at[target], sum_sems[1].at[chip], 2 * target + core
        )

    def own_sum():
        return pltpu.make_async_copy(summed.at[:, chip], landed.at[chip], sum_sems[1].at[chip])

    swap_sems = take(2)
    sum_sems = take(2)
    dq_begin, dq_end = give_back(chip, core, dq, q_landed, *take(2))

    def key_grads(step):
        target = (chip + step) % CHIPS
        weights = jnp.exp2(logits(target) * FACTOR - stat[NORM])
        readout_dots = nt(keys_of(kv.at[1], target), flat(r))
        slopes = (weights * (readout_dots - stat[ROW_DOTS])).astype(jnp.bfloat16)
        key_part = (SCALE * nn(slopes, flat(q))).astype(jnp.bfloat16)
        value_part = nn(weights.astype(jnp.bfloat16), flat(r)).astype(jnp.bfloat16)
        dkv[0, target] = key_part.reshape(2, HD, HD)
        dkv[1, target] = value_part.reshape(2, HD, HD)
        swap(target).start()
        dq_acc[...] += tn(keys_of(kv.at[0], target), slopes)

    def add_partner(step):
        target = (chip + step) % CHIPS
        swap(target).wait_recv()
        summed[:, target] = (
            dkv[:, target, core].astype(jnp.float32) + other[:, target].astype(jnp.float32)
        ).astype(jnp.bfloat16)

        @pl.when(step > 0)
        def _():
            out_copy(target).start()

        @pl.when(step == 0)
        def _():
            own_sum().start()

    @pl.when(busy)
    def _():
        stat[NORM] = stat[TOP] * FACTOR + jnp.log2(stat[TOTAL])
        stat[ROW_DOTS] = stat[WEIGHTED] / stat[TOTAL]
        key_grads(0)

        def go(step, carry):
            key_grads(step)
            add_partner(step - 1)
            return carry

        lax.fori_loop(1, CHIPS, go, 0)
        add_partner(CHIPS - 1)
        dq[...] = (SCALE * dq_acc[...]).T.astype(jnp.bfloat16).reshape(SLOTS, HD, HD)

    dq_begin()
    gather.sent()
    kv_sent()
    q_sent()
    r_sent()

    def come(step, carry):
        source = (chip + CHIPS - step) % CHIPS

        @pl.when(jnp.logical_and(source < BUSY, step > 0))
        def _():
            remote(
                summed.at[:, 0], landed.at[source], sum_sems[0].at[0], sum_sems[1].at[source], partner
            ).wait_recv()

        @pl.when(jnp.logical_and(source < BUSY, step == 0))
        def _():
            own_sum().wait()

        return carry

    lax.fori_loop(0, CHIPS, come, 0)
    for h in range(HEADS):
        span = slice(h * HD, (h + 1) * HD)
        total = landed[3 * h].astype(jnp.float32) + landed[3 * h + 1].astype(jnp.float32)
        total = (total + landed[3 * h + 2].astype(jnp.float32)).astype(jnp.bfloat16)
        grads[1, :, span] = total[0]
        grads[2, :, span] = total[1]
    dq_end()
    for h in range(HEADS):
        grads[0, :, h * HD : (h + 1) * HD] = q_landed[h]

    regather = Gather(gx_all, *take(3))
    qd_begin, qd_arrived, qd_sent = deal_queries(chip, core, qd_heads, qd, *take(2))
    kvd_begin, kvd_consume, kvd_sent = deal_keys(chip, core, kvd_heads, dots, *take(4))
    via_send, via_recv, direct_send, direct_recv, mix_send, mix_recv = take(6)
    depth = regather.width

    def near_far(panel):
        return (regather.right, regather.left) if panel % 2 == 0 else (regather.left, regather.right)

    def part(layer, panel):
        return parts.at[regather.rows(layer), regather.columns(panel)]

    def piece(ref, panel):
        return ref.at[:, regather.columns(panel)]

    def via_copy(panel):
        return remote(
            part(regather.across, panel), piece(via, panel), via_send.at[panel], via_recv.at[panel],
            near_far(panel)[1], "head",
        )

    def direct_copy(panel):
        target = near_far(panel)[0]
        return remote(
            part(target, panel), piece(direct, panel), direct_send.at[panel], direct_recv.at[panel], target, "head"
        )

    def mix_copy(panel):
        return remote(
            piece(mix_out, panel), piece(mixed, panel), mix_send.at[panel], mix_recv.at[panel],
            near_far(panel)[1], "head",
        )

    def share(panel):
        span = slice(panel * depth, (panel + 1) * depth)
        total = nt(grads[0], w_ref[0, span, :])
        total += nt(grads[1], w_ref[1, span, :])
        total += nt(grads[2], w_ref[2, span, :])
        parts[:, span] = total.astype(jnp.bfloat16)
        via_copy(panel).start()
        direct_copy(panel).start()

    def mix(panel):
        span = slice(panel * depth, (panel + 1) * depth)
        via_copy(panel).wait_recv()
        mine = parts[regather.rows(near_far(panel)[1]), span]
        mix_out[:, span] = (via[:, span].astype(jnp.float32) + mine.astype(jnp.float32)).astype(jnp.bfloat16)
        mix_copy(panel).start()

    def settle(panel):
        span = slice(panel * depth, (panel + 1) * depth)
        direct_copy(panel).wait_recv()
        mix_copy(panel).wait_recv()
        mine = parts[regather.rows(regather.layer), span].astype(jnp.float32)
        total = mine + direct[:, span].astype(jnp.float32) + mixed[:, span].astype(jnp.float32)
        total = total.astype(jnp.bfloat16)
        gx_ref[:, span] = total
        gx_all[regather.rows(regather.layer), span] = total
        regather.start(panel)

    def absorb(panel):
        regather.rest(panel)
        add_panel(totals, gx_all, w_ref, panel, panel == 0)

    stages = ((share, 0), (mix, 1), (settle, 3), (regather.relay, 4), (absorb, 6))
    for step in range(PANELS + 6):
        for stage, lag in stages:
            if 0 <= step - lag < PANELS:
                stage(step - lag)
    split_heads(totals, qd_heads, kvd_heads)
    qd_begin()
    kvd_begin()

    def tangent(source):
        keys, values = keys_of(kv.at[0], source), keys_of(kv.at[1], source)
        key_dots, value_dots = keys_of(dots.at[0], source), keys_of(dots.at[1], source)
        weights = jnp.exp2(logits(source) * FACTOR - stat[NORM])
        moved = nt(jnp.concatenate([keys, key_dots], axis=1), jnp.concatenate([flat(qd), flat(q)], axis=1))
        turned = weights * (moved * SCALE)
        dq_acc[...] += tn(values, turned.astype(jnp.bfloat16))
        plain[...] += tn(jnp.concatenate([values, value_dots], axis=1), weights.astype(jnp.bfloat16))
        stat[CURVE] += turned.sum(axis=0, keepdims=True)

    qd_arrived()

    @pl.when(busy)
    def _():
        dq_acc[...] = jnp.zeros_like(dq_acc)
        plain[...] = jnp.zeros_like(plain)

    kvd_consume(tangent)
    pen_begin, pen_end = give_back(chip, core, penalty, p_landed, *take(2))

    @pl.when(busy)
    def _():
        total = dq_acc[...] + plain[HD:, :] - stat[CURVE] * plain[:HD, :]
        penalty[...] = total.T.astype(jnp.bfloat16).reshape(SLOTS, HD, HD)

    pen_begin()

    @pl.when(busy)
    def _():
        def gone(step, carry):
            target = (chip + step) % CHIPS
            swap(target).wait_send()

            @pl.when(step > 0)
            def _():
                out_copy(target).wait_send()

            return carry

        lax.fori_loop(0, CHIPS, gone, 0)

    regather.sent()
    for panel in range(PANELS):
        via_copy(panel).wait_send()
        direct_copy(panel).wait_send()
        mix_copy(panel).wait_send()
    kvd_sent()
    qd_sent()
    pen_end()
    for h in range(HEADS):
        pen_ref[:, h * HD : (h + 1) * HD] = p_landed[h]


def on_device(clip_tokens, w_qkv, readout, token_latent_frame, frame_mask):
    panel_rows, width = clip_tokens.shape
    tokens, columns = readout.shape

    def low(*shape):
        return pltpu.VMEM(shape, jnp.bfloat16)

    def wide(*shape):
        return pltpu.VMEM(shape, jnp.float32)

    gather_sems = [DMA((2, PANELS)), DMA((PANELS,)), DMA((3, PANELS))]
    query_sems = [DMA((HEADS,)), DMA((SLOTS,))]
    back_sems = [DMA((SLOTS,)), DMA((HEADS,))]
    chip_sems = [DMA((CHIPS,))] * 4
    scratch = dict(
        w_ref=low(*w_qkv.shape),
        x_all=low(tokens, width),
        gx_all=low(tokens, width),
        totals=wide(3, tokens, columns),
        q_heads=low(HEADS, HD, HD),
        kv_heads=low(2, HEADS, HD, HD),
        r_heads=low(HEADS, HD, HD),
        qd_heads=low(HEADS, HD, HD),
        kvd_heads=low(2, HEADS, HD, HD),
        kv=low(2, CHIPS, 2, HD, HD),
        dots=low(2, CHIPS, 2, HD, HD),
        q=low(SLOTS, HD, HD),
        r=low(SLOTS, HD, HD),
        qd=low(SLOTS, HD, HD),
        key_hot=low(TOKENS, HD),
        row_bar=low(ROWS, HD),
        barred=wide(HD, HD),
        stat=wide(6, 1, ROWS),
        dkv=low(2, CHIPS, 2, HD, HD),
        dq_acc=wide(HD, ROWS),
        dq=low(SLOTS, HD, HD),
        penalty=low(SLOTS, HD, HD),
        other=low(2, CHIPS, HD, HD),
        summed=low(2, CHIPS, HD, HD),
        landed=low(CHIPS, 2, HD, HD),
        q_landed=low(HEADS, HD, HD),
        p_landed=low(HEADS, HD, HD),
        plain=wide(2 * HD, ROWS),
        grads=low(3, tokens, columns),
        parts=low(tokens, width),
        via=low(panel_rows, width),
        direct=low(panel_rows, width),
        mixed=low(panel_rows, width),
        mix_out=low(panel_rows, width),
        w_sems=DMA((PANELS,)),
    )
    sems = (
        gather_sems + query_sems * 2 + chip_sems + chip_sems + back_sems
        + gather_sems + query_sems + chip_sems + [DMA((PANELS,))] * 6 + back_sems
    )
    return pl.pallas_call(
        whole_kernel,
        out_shape=(
            jax.ShapeDtypeStruct((panel_rows, width), jnp.bfloat16),
            jax.ShapeDtypeStruct((tokens, columns), jnp.bfloat16),
        ),
        in_specs=[VMEM, HBM, VMEM, VMEM, VMEM],
        out_specs=(VMEM, VMEM),
        scratch_shapes=list(scratch.values()) + sems,
        compiler_params=pltpu.CompilerParams(
            collective_id=0, has_side_effects=True, vmem_limit_bytes=58 << 20
        ),
        name="whole",
    )(clip_tokens, w_qkv, readout, token_latent_frame.reshape(-1, HD), frame_mask)


def solution(mesh):
    return jax.shard_map(
        on_device,
        mesh=mesh,
        in_specs=(P(("seq", "head"), None), P(None, None, "head"), P("seq", "head"), P(), P()),
        out_specs=(P(("seq", "head"), None), P("seq", "head")),
        check_vma=False,
    )
```

```python
import functools
import math

import jax
import jax.numpy as jnp
from jax import lax
from jax.experimental import pallas as pl
from jax.experimental.pallas import tpu as pltpu
from jax.sharding import PartitionSpec as P

HD = 128
MESH = pl.DeviceIdType.MESH
LOG2E = math.log2(math.e)
BARRED = -1e30

CHIPS = 16
BUSY = 15
HEADS = 5
SLOTS = 6
LAG = 2


def start_of(third):
    return (CHIPS * third + 2) // 3


def third_of(chip):
    return (chip * 3) // CHIPS


def place():
    me = lax.axis_index("seq")
    return me // 2, me % 2


PANELS = 10
AHEAD = 4
LAYERS = 4


def enter(chip, core, layers=False):
    barrier = pltpu.get_barrier_semaphore()

    def greet(step, carry):
        peer = (chip + step) % CHIPS
        pl.semaphore_signal(barrier, inc=1, device_id={"seq": 2 * peer + core}, device_id_type=MESH)
        return carry

    lax.fori_loop(1, CHIPS, greet, 0)
    pl.semaphore_signal(barrier, inc=1, device_id={"seq": 2 * chip + 1 - core}, device_id_type=MESH)
    if layers:
        layer = lax.axis_index("head")
        for step in (1, LAYERS - 1):
            pl.semaphore_signal(
                barrier, inc=1, device_id={"head": (layer + step) % LAYERS}, device_id_type=MESH
            )
    pl.semaphore_wait(barrier, CHIPS + (2 if layers else 0))


def remote(src, dst, send_sem, recv_sem, device, axis="seq"):
    return pltpu.make_async_remote_copy(
        src_ref=src,
        dst_ref=dst,
        send_sem=send_sem,
        recv_sem=recv_sem,
        device_id={axis: device},
        device_id_type=MESH,
    )


def deal_queries(chip, core, src, dst, send, recv):
    third = third_of(chip)
    slot = chip - start_of(third)
    own_third = chip % 3
    first = start_of(own_third)
    count = start_of(own_third + 1) - first
    partner = 2 * chip + 1 - core

    def copy(h):
        return remote(src.at[h], dst.at[slot], send.at[h], recv.at[slot], 2 * (3 * h + third) + core)

    def own():
        return pltpu.make_async_copy(src.at[chip // 3], dst.at[slot], recv.at[slot])

    def begin():
        def go(h, carry):
            @pl.when(3 * h + third != chip)
            def _():
                copy(h).start()

            @pl.when(3 * h + third == chip)
            def _():
                own().start()

            return carry

        lax.fori_loop(0, HEADS, go, 0)

    def arrived():
        @pl.when(chip < BUSY)
        def _():
            def come(n, carry):
                @pl.when(first + n != chip)
                def _():
                    remote(src.at[0], dst.at[n], send.at[0], recv.at[n], partner).wait_recv()

                @pl.when(first + n == chip)
                def _():
                    own().wait()

                return carry

            lax.fori_loop(0, count, come, 0)

            @pl.when(count < SLOTS)
            def _():
                dst[SLOTS - 1] = jnp.zeros_like(dst[SLOTS - 1])

    def sent():
        def gone(h, carry):
            @pl.when(3 * h + third != chip)
            def _():
                copy(h).wait_send()

            return carry

        lax.fori_loop(0, HEADS, gone, 0)

    return begin, arrived, sent


def deal_keys(chip, core, src, dst, kv_send, kv_recv, pass_send, pass_recv):
    partner = 2 * chip + 1 - core

    def copy(d):
        return remote(src.at[:, d // 3], dst.at[:, chip, core], kv_send.at[d], kv_recv.at[chip], 2 * d + core)

    def own():
        return pltpu.make_async_copy(src.at[:, chip // 3], dst.at[:, chip, core], kv_recv.at[chip])

    def pass_copy(source, half):
        return remote(
            dst.at[:, source, half], dst.at[:, source, half], pass_send.at[source], pass_recv.at[source], partner
        )

    def begin():
        def go(step, carry):
            d = (chip + step) % CHIPS

            @pl.when(jnp.logical_and(d < BUSY, step > 0))
            def _():
                copy(d).start()

            @pl.when(jnp.logical_and(d < BUSY, step == 0))
            def _():
                own().start()

            return carry

        lax.fori_loop(0, CHIPS, go, 0)

    def source_of(step):
        return (chip + CHIPS - step) % CHIPS

    def arrive(step):
        source = source_of(step)

        @pl.when(step > 0)
        def _():
            remote(
                src.at[:, 0], dst.at[:, source, core], kv_send.at[0], kv_recv.at[source], partner
            ).wait_recv()

        @pl.when(step == 0)
        def _():
            own().wait()

        pass_copy(source, core).start()

    def use(step, body):
        source = source_of(step)
        pass_copy(source, 1 - core).wait_recv()
        body(source)

    def consume(body):
        @pl.when(chip < BUSY)
        def _():
            def first(step, carry):
                arrive(step)
                return carry

            def both(step, carry):
                arrive(step)
                use(step - LAG, body)
                return carry

            def last(step, carry):
                use(step, body)
                return carry

            lax.fori_loop(0, LAG, first, 0)
            lax.fori_loop(LAG, CHIPS, both, 0)
            lax.fori_loop(CHIPS - LAG, CHIPS, last, 0)

    def sent():
        @pl.when(chip < BUSY)
        def _():
            def passed(step, carry):
                pass_copy(source_of(step), core).wait_send()
                return carry

            lax.fori_loop(0, CHIPS, passed, 0)

        def gone(step, carry):
            d = (chip + step) % CHIPS

            @pl.when(d < BUSY)
            def _():
                copy(d).wait_send()

            return carry

        lax.fori_loop(1, CHIPS, gone, 0)

    return begin, consume, sent


VMEM = pl.BlockSpec(memory_space=pltpu.VMEM)
HBM = pl.BlockSpec(memory_space=pl.ANY)
DMA = pltpu.SemaphoreType.DMA


class Gather:
    def __init__(self, rows_ref, own_send, pass_send, recv):
        self.ref, self.own_send, self.pass_send, self.recv = rows_ref, own_send, pass_send, recv
        self.layer = lax.axis_index("head")
        self.right, self.left = (self.layer + 1) % LAYERS, (self.layer + LAYERS - 1) % LAYERS
        self.across = (self.layer + 2) % LAYERS
        self.height = rows_ref.shape[0] // LAYERS
        self.width = rows_ref.shape[1] // PANELS

    def rows(self, layer):
        return pl.ds(pl.multiple_of(layer * self.height, self.height), self.height)

    def columns(self, panel):
        return pl.ds(panel * self.width, self.width)

    def block(self, layer, panel):
        return self.ref.at[self.rows(layer), self.columns(panel)]

    def copy(self, layer, panel, send, kind, target):
        block = self.block(layer, panel)
        return remote(block, block, send, self.recv.at[kind, panel], target, "head")

    def own(self, panel):
        return (
            self.copy(self.layer, panel, self.own_send.at[0, panel], 0, self.right),
            self.copy(self.layer, panel, self.own_send.at[1, panel], 1, self.left),
        )

    def start(self, panel):
        for copy in self.own(panel):
            copy.start()

    def passing(self, panel):
        if panel % 2 == 0:
            return self.copy(self.left, panel, self.pass_send.at[panel], 2, self.right)
        return self.copy(self.right, panel, self.pass_send.at[panel], 2, self.left)

    def relay(self, panel):
        if panel % 2 == 0:
            self.copy(self.left, panel, self.pass_send.at[panel], 0, self.right).wait_recv()
        else:
            self.copy(self.right, panel, self.pass_send.at[panel], 1, self.left).wait_recv()
        self.passing(panel).start()

    def rest(self, panel):
        if panel % 2 == 0:
            self.copy(self.right, panel, self.pass_send.at[panel], 1, self.left).wait_recv()
        else:
            self.copy(self.left, panel, self.pass_send.at[panel], 0, self.right).wait_recv()
        self.copy(self.across, panel, self.pass_send.at[panel], 2, self.right).wait_recv()

    def sent(self):
        for panel in range(PANELS):
            for copy in self.own(panel):
                copy.wait_send()
            self.passing(panel).wait_send()


def panel_of_w(w_hbm, w_ref, sems, panel):
    depth = w_ref.shape[1] // PANELS
    rows = pl.ds(panel * depth, depth)
    return pltpu.make_async_copy(w_hbm.at[:, rows], w_ref.at[:, rows], sems.at[panel])


def add_panel(totals, rows_ref, w_ref, panel, first):
    depth = w_ref.shape[1] // PANELS
    span = slice(panel * depth, (panel + 1) * depth)
    for c in range(3):
        term = jnp.dot(rows_ref[:, span], w_ref[c, span, :], preferred_element_type=jnp.float32)
        totals[c] = term if first else totals[c] + term


def split_heads(totals, q_heads, kv_heads):
    for h in range(HEADS):
        span = slice(h * HD, (h + 1) * HD)
        q_heads[h] = totals[0, :, span].astype(jnp.bfloat16)
        kv_heads[0, h] = totals[1, :, span].astype(jnp.bfloat16)
        kv_heads[1, h] = totals[2, :, span].astype(jnp.bfloat16)


def give_back(chip, core, src, dst, send, recv):
    own_third = chip % 3
    first = start_of(own_third)
    count = start_of(own_third + 1) - first
    third = third_of(chip)
    own_head = chip // 3

    def out_copy(n):
        return remote(src.at[n], dst.at[own_head], send.at[n], recv.at[own_head], 2 * (first + n) + core)

    def own():
        return pltpu.make_async_copy(src.at[chip - first], dst.at[own_head], recv.at[own_head])

    def begin():
        @pl.when(chip < BUSY)
        def _():
            def go(n, carry):
                @pl.when(first + n != chip)
                def _():
                    out_copy(n).start()

                @pl.when(first + n == chip)
                def _():
                    own().start()

                return carry

            lax.fori_loop(0, count, go, 0)

    def end():
        def come(h, carry):
            @pl.when(3 * h + third != chip)
            def _():
                remote(src.at[0], dst.at[h], send.at[0], recv.at[h], 2 * chip + 1 - core).wait_recv()

            @pl.when(3 * h + third == chip)
            def _():
                own().wait()

            return carry

        lax.fori_loop(0, HEADS, come, 0)

        @pl.when(chip < BUSY)
        def _():
            def gone(n, carry):
                @pl.when(first + n != chip)
                def _():
                    out_copy(n).wait_send()

                return carry

            lax.fori_loop(0, count, gone, 0)

    return begin, end


TOKENS = 4096
ROWS = SLOTS * HD
CHUNK = 2 * HD
SCALE = HD ** (-0.5)
FACTOR = SCALE * LOG2E


def nt(left, right):
    return lax.dot_general(left, right, (((1,), (1,)), ((), ())), preferred_element_type=jnp.float32)


def nn(left, right):
    return lax.dot_general(left, right, (((1,), (0,)), ((), ())), preferred_element_type=jnp.float32)


def tn(left, right):
    return lax.dot_general(left, right, (((0,), (0,)), ((), ())), preferred_element_type=jnp.float32)


def mask_sides(frames_ref, mask_ref, key_hot, row_bar, barred, first, core):
    frames = frames_ref[...]
    count = mask_ref.shape[0]
    lane = lax.broadcasted_iota(jnp.int32, (1, HD), 1)
    start = jnp.full((1, HD), TOKENS, jnp.int32)
    end = jnp.full((1, HD), TOKENS, jnp.int32)
    for f in range(count):
        below = jnp.sum((frames < f).astype(jnp.float32), keepdims=True).astype(jnp.int32)
        start = jnp.where(lane == f, below, start)
        end = jnp.where(lane == f - 1, below, end)

    def hot(tokens):
        return jnp.where(jnp.logical_and(tokens >= start, tokens < end), 1.0, 0.0).astype(jnp.bfloat16)

    row = lax.broadcasted_iota(jnp.int32, (HD, HD), 0)

    def fill(block, carry):
        key_hot[pl.ds(pl.multiple_of(block * HD, HD), HD), :] = hot(row + block * HD)
        return carry

    lax.fori_loop(0, TOKENS // HD, fill, 0)
    barred[...] = jnp.zeros_like(barred)
    barred[:count, :count] = jnp.where(mask_ref[...] == 1, 0.0, BARRED)
    table = barred[...].astype(jnp.bfloat16)
    for n in range(SLOTS):
        own = hot(row + (2 * (first + n) + core) * HD)
        row_bar[n * HD : (n + 1) * HD, :] = nn(own, table).astype(jnp.bfloat16)


TOP, TOTAL, WEIGHTED, NORM, ROW_DOTS, CURVE = range(6)


def whole_kernel(
    x_ref, w_hbm, readout_ref, frames_ref, mask_ref, gx_ref, pen_ref,
    w_ref, x_all, gx_all, totals, q_heads, kv_heads, r_heads, qd_heads, kvd_heads,
    kv, dots, q, r, qd, key_hot, row_bar, barred, stat,
    dkv, dq_acc, dq, penalty, other, summed, landed, q_landed, p_landed, plain, grads,
    parts, via, direct, mixed, mix_out, kept,
    w_sems, *sems
):
    sems = list(sems)

    def take(n):
        taken = sems[:n]
        del sems[:n]
        return taken

    chip, core = place()
    partner = 2 * chip + 1 - core
    busy = chip < BUSY
    first = start_of(chip % 3)
    for panel in range(PANELS):
        panel_of_w(w_hbm, w_ref, w_sems, panel).start()
    gather = Gather(x_all, *take(3))
    x_all[gather.rows(gather.layer), :] = x_ref[...]
    for h in range(HEADS):
        r_heads[h] = readout_ref[:, h * HD : (h + 1) * HD]
    enter(chip, core, layers=True)
    for panel in range(PANELS):
        gather.start(panel)
    r_begin, r_arrived, r_sent = deal_queries(chip, core, r_heads, r, *take(2))
    q_begin, q_arrived, q_sent = deal_queries(chip, core, q_heads, q, *take(2))
    kv_begin, kv_consume, kv_sent = deal_keys(chip, core, kv_heads, kv, *take(4))
    r_begin()
    mask_sides(frames_ref, mask_ref, key_hot, row_bar, barred, first, core)

    for panel in range(AHEAD):
        gather.relay(panel)
    for panel in range(PANELS):
        if panel + AHEAD < PANELS:
            gather.relay(panel + AHEAD)
        gather.rest(panel)
        panel_of_w(w_hbm, w_ref, w_sems, panel).wait()
        add_panel(totals, x_all, w_ref, panel, panel == 0)
    split_heads(totals, q_heads, kv_heads)
    q_begin()
    kv_begin()

    def keys_of(array, source):
        return array[source].reshape(CHUNK, HD)

    def flat(array):
        return array[...].reshape(ROWS, HD)

    def logits(source):
        hot = key_hot[pl.ds(pl.multiple_of(source * CHUNK, CHUNK), CHUNK), :]
        return nt(
            jnp.concatenate([keys_of(kv.at[0], source), hot], axis=1),
            jnp.concatenate([flat(q), row_bar[...]], axis=1),
        )

    def stats(source):
        raw = logits(source)
        readout_dots = nt(keys_of(kv.at[1], source), flat(r))
        top = stat[TOP]
        new_top = jnp.maximum(top, raw.max(axis=0, keepdims=True))
        weights = jnp.exp2((raw - new_top) * FACTOR)
        shrink = jnp.exp2((top - new_top) * FACTOR)
        stat[TOP] = new_top
        stat[TOTAL] = stat[TOTAL] * shrink + weights.sum(axis=0, keepdims=True)
        stat[WEIGHTED] = stat[WEIGHTED] * shrink + (weights * readout_dots).sum(axis=0, keepdims=True)

    q_arrived()
    r_arrived()

    @pl.when(busy)
    def _():
        stat[...] = jnp.zeros_like(stat)
        stat[TOP] = jnp.full((1, ROWS), BARRED, jnp.float32)
        dq_acc[...] = jnp.zeros_like(dq_acc)

    kv_consume(stats)

    def swap(target):
        x_send, x_recv = swap_sems
        return remote(
            dkv.at[:, target, 1 - core], other.at[:, target], x_send.at[target], x_recv.at[target], partner
        )

    def out_copy(target):
        return remote(
            summed.at[:, target], landed.at[chip], sum_sems[0].at[target], sum_sems[1].at[chip], 2 * target + core
        )

    def own_sum():
        return pltpu.make_async_copy(summed.at[:, chip], landed.at[chip], sum_sems[1].at[chip])

    swap_sems = take(2)
    sum_sems = take(2)
    dq_begin, dq_end = give_back(chip, core, dq, q_landed, *take(2))

    def key_grads(step):
        target = (chip + step) % CHIPS
        weights = jnp.exp2(logits(target) * FACTOR - stat[NORM])
        weights_low = weights.astype(jnp.bfloat16)
        kept[target] = weights_low
        readout_dots = nt(keys_of(kv.at[1], target), flat(r))
        slopes = (weights * (readout_dots - stat[ROW_DOTS])).astype(jnp.bfloat16)
        key_part = (SCALE * nn(slopes, flat(q))).astype(jnp.bfloat16)
        value_part = nn(weights_low, flat(r)).astype(jnp.bfloat16)
        dkv[0, target] = key_part.reshape(2, HD, HD)
        dkv[1, target] = value_part.reshape(2, HD, HD)
        swap(target).start()
        dq_acc[...] += tn(keys_of(kv.at[0], target), slopes)

    def add_partner(step):
        target = (chip + step) % CHIPS
        swap(target).wait_recv()
        summed[:, target] = (
            dkv[:, target, core].astype(jnp.float32) + other[:, target].astype(jnp.float32)
        ).astype(jnp.bfloat16)

        @pl.when(step > 0)
        def _():
            out_copy(target).start()

        @pl.when(step == 0)
        def _():
            own_sum().start()

    @pl.when(busy)
    def _():
        stat[NORM] = stat[TOP] * FACTOR + jnp.log2(stat[TOTAL])
        stat[ROW_DOTS] = stat[WEIGHTED] / stat[TOTAL]
        key_grads(0)

        def go(step, carry):
            key_grads(step)
            add_partner(step - 1)
            return carry

        lax.fori_loop(1, CHIPS, go, 0)
        dq[...] = (SCALE * dq_acc[...]).T.astype(jnp.bfloat16).reshape(SLOTS, HD, HD)

    dq_begin()

    @pl.when(busy)
    def _():
        add_partner(CHIPS - 1)

    gather.sent()
    kv_sent()
    q_sent()
    r_sent()

    def come(step, carry):
        source = (chip + CHIPS - step) % CHIPS

        @pl.when(jnp.logical_and(source < BUSY, step > 0))
        def _():
            remote(
                summed.at[:, 0], landed.at[source], sum_sems[0].at[0], sum_sems[1].at[source], partner
            ).wait_recv()

        @pl.when(jnp.logical_and(source < BUSY, step == 0))
        def _():
            own_sum().wait()

        return carry

    lax.fori_loop(0, CHIPS, come, 0)
    for h in range(HEADS):
        span = slice(h * HD, (h + 1) * HD)
        total = landed[3 * h].astype(jnp.float32) + landed[3 * h + 1].astype(jnp.float32)
        total = (total + landed[3 * h + 2].astype(jnp.float32)).astype(jnp.bfloat16)
        grads[1, :, span] = total[0]
        grads[2, :, span] = total[1]
    dq_end()
    for h in range(HEADS):
        grads[0, :, h * HD : (h + 1) * HD] = q_landed[h]

    regather = Gather(gx_all, *take(3))
    qd_begin, qd_arrived, qd_sent = deal_queries(chip, core, qd_heads, qd, *take(2))
    kvd_begin, kvd_consume, kvd_sent = deal_keys(chip, core, kvd_heads, dots, *take(4))
    via_send, via_recv, direct_send, direct_recv, mix_send, mix_recv = take(6)
    depth = regather.width

    def near_far(panel):
        return (regather.right, regather.left) if panel % 2 == 0 else (regather.left, regather.right)

    def part(layer, panel):
        return parts.at[regather.rows(layer), regather.columns(panel)]

    def piece(ref, panel):
        return ref.at[:, regather.columns(panel)]

    def via_copy(panel):
        return remote(
            part(regather.across, panel), piece(via, panel), via_send.at[panel], via_recv.at[panel],
            near_far(panel)[1], "head",
        )

    def direct_copy(panel):
        target = near_far(panel)[0]
        return remote(
            part(target, panel), piece(direct, panel), direct_send.at[panel], direct_recv.at[panel], target, "head"
        )

    def mix_copy(panel):
        return remote(
            piece(mix_out, panel), piece(mixed, panel), mix_send.at[panel], mix_recv.at[panel],
            near_far(panel)[1], "head",
        )

    def share(panel):
        span = slice(panel * depth, (panel + 1) * depth)
        total = nt(grads[0], w_ref[0, span, :])
        total += nt(grads[1], w_ref[1, span, :])
        total += nt(grads[2], w_ref[2, span, :])
        parts[:, span] = total.astype(jnp.bfloat16)
        via_copy(panel).start()
        direct_copy(panel).start()

    def mix(panel):
        span = slice(panel * depth, (panel + 1) * depth)
        via_copy(panel).wait_recv()
        mine = parts[regather.rows(near_far(panel)[1]), span]
        mix_out[:, span] = (via[:, span].astype(jnp.float32) + mine.astype(jnp.float32)).astype(jnp.bfloat16)
        mix_copy(panel).start()

    def settle(panel):
        span = slice(panel * depth, (panel + 1) * depth)
        direct_copy(panel).wait_recv()
        mix_copy(panel).wait_recv()
        mine = parts[regather.rows(regather.layer), span].astype(jnp.float32)
        total = mine + direct[:, span].astype(jnp.float32) + mixed[:, span].astype(jnp.float32)
        total = total.astype(jnp.bfloat16)
        gx_ref[:, span] = total
        gx_all[regather.rows(regather.layer), span] = total
        regather.start(panel)

    def absorb(panel):
        regather.rest(panel)
        add_panel(totals, gx_all, w_ref, panel, panel == 0)

    stages = ((share, 0), (mix, 3), (settle, 6), (regather.relay, 9), (absorb, 12))
    for step in range(PANELS + stages[-1][1]):
        for stage, lag in stages:
            if 0 <= step - lag < PANELS:
                stage(step - lag)
    split_heads(totals, qd_heads, kvd_heads)
    qd_begin()
    kvd_begin()

    def tangent(source):
        keys, values = keys_of(kv.at[0], source), keys_of(kv.at[1], source)
        key_dots, value_dots = keys_of(dots.at[0], source), keys_of(dots.at[1], source)
        weights_low = kept[source]
        moved = nt(jnp.concatenate([keys, key_dots], axis=1), jnp.concatenate([flat(qd), flat(q)], axis=1))
        turned = weights_low.astype(jnp.float32) * (moved * SCALE)
        dq_acc[...] += tn(values, turned.astype(jnp.bfloat16))
        plain[...] += tn(jnp.concatenate([values, value_dots], axis=1), weights_low)
        stat[CURVE] += turned.sum(axis=0, keepdims=True)

    qd_arrived()

    @pl.when(busy)
    def _():
        dq_acc[...] = jnp.zeros_like(dq_acc)
        plain[...] = jnp.zeros_like(plain)

    kvd_consume(tangent)
    pen_begin, pen_end = give_back(chip, core, penalty, p_landed, *take(2))

    @pl.when(busy)
    def _():
        total = dq_acc[...] + plain[HD:, :] - stat[CURVE] * plain[:HD, :]
        penalty[...] = total.T.astype(jnp.bfloat16).reshape(SLOTS, HD, HD)

    pen_begin()

    @pl.when(busy)
    def _():
        def gone(step, carry):
            target = (chip + step) % CHIPS
            swap(target).wait_send()

            @pl.when(step > 0)
            def _():
                out_copy(target).wait_send()

            return carry

        lax.fori_loop(0, CHIPS, gone, 0)

    regather.sent()
    for panel in range(PANELS):
        via_copy(panel).wait_send()
        direct_copy(panel).wait_send()
        mix_copy(panel).wait_send()
    kvd_sent()
    qd_sent()
    pen_end()
    for h in range(HEADS):
        pen_ref[:, h * HD : (h + 1) * HD] = p_landed[h]


def on_device(clip_tokens, w_qkv, readout, token_latent_frame, frame_mask):
    panel_rows, width = clip_tokens.shape
    tokens, columns = readout.shape

    def low(*shape):
        return pltpu.VMEM(shape, jnp.bfloat16)

    def wide(*shape):
        return pltpu.VMEM(shape, jnp.float32)

    gather_sems = [DMA((2, PANELS)), DMA((PANELS,)), DMA((3, PANELS))]
    query_sems = [DMA((HEADS,)), DMA((SLOTS,))]
    back_sems = [DMA((SLOTS,)), DMA((HEADS,))]
    chip_sems = [DMA((CHIPS,))] * 4
    scratch = dict(
        w_ref=low(*w_qkv.shape),
        x_all=low(tokens, width),
        gx_all=low(tokens, width),
        totals=wide(3, tokens, columns),
        q_heads=low(HEADS, HD, HD),
        kv_heads=low(2, HEADS, HD, HD),
        r_heads=low(HEADS, HD, HD),
        qd_heads=low(HEADS, HD, HD),
        kvd_heads=low(2, HEADS, HD, HD),
        kv=low(2, CHIPS, 2, HD, HD),
        dots=low(2, CHIPS, 2, HD, HD),
        q=low(SLOTS, HD, HD),
        r=low(SLOTS, HD, HD),
        qd=low(SLOTS, HD, HD),
        key_hot=low(TOKENS, HD),
        row_bar=low(ROWS, HD),
        barred=wide(HD, HD),
        stat=wide(6, 1, ROWS),
        dkv=low(2, CHIPS, 2, HD, HD),
        dq_acc=wide(HD, ROWS),
        dq=low(SLOTS, HD, HD),
        penalty=low(SLOTS, HD, HD),
        other=low(2, CHIPS, HD, HD),
        summed=low(2, CHIPS, HD, HD),
        landed=low(CHIPS, 2, HD, HD),
        q_landed=low(HEADS, HD, HD),
        p_landed=low(HEADS, HD, HD),
        plain=wide(2 * HD, ROWS),
        grads=low(3, tokens, columns),
        parts=low(tokens, width),
        via=low(panel_rows, width),
        direct=low(panel_rows, width),
        mixed=low(panel_rows, width),
        mix_out=low(panel_rows, width),
        kept=low(CHIPS, CHUNK, ROWS),
        w_sems=DMA((PANELS,)),
    )
    sems = (
        gather_sems + query_sems * 2 + chip_sems + chip_sems + back_sems
        + gather_sems + query_sems + chip_sems + [DMA((PANELS,))] * 6 + back_sems
    )
    return pl.pallas_call(
        whole_kernel,
        out_shape=(
            jax.ShapeDtypeStruct((panel_rows, width), jnp.bfloat16),
            jax.ShapeDtypeStruct((tokens, columns), jnp.bfloat16),
        ),
        in_specs=[VMEM, HBM, VMEM, VMEM, VMEM],
        out_specs=(VMEM, VMEM),
        scratch_shapes=list(scratch.values()) + sems,
        compiler_params=pltpu.CompilerParams(
            collective_id=0, has_side_effects=True, vmem_limit_bytes=58 << 20
        ),
        name="whole",
    )(clip_tokens, w_qkv, readout, token_latent_frame.reshape(-1, HD), frame_mask)


def solution(mesh):
    return jax.shard_map(
        on_device,
        mesh=mesh,
        in_specs=(P(("seq", "head"), None), P(None, None, "head"), P("seq", "head"), P(), P()),
        out_specs=(P(("seq", "head"), None), P("seq", "head")),
        check_vma=False,
    )
```

```python
import functools
import math

import jax
import jax.numpy as jnp
from jax import lax
from jax.experimental import pallas as pl
from jax.experimental.pallas import tpu as pltpu
from jax.sharding import PartitionSpec as P

HD = 128
MESH = pl.DeviceIdType.MESH
LOG2E = math.log2(math.e)
BARRED = -1e30

CHIPS = 16
BUSY = 15
HEADS = 5
SLOTS = 6
LAG = 2


def start_of(third):
    return (CHIPS * third + 2) // 3


def third_of(chip):
    return (chip * 3) // CHIPS


def place():
    me = lax.axis_index("seq")
    return me // 2, me % 2


PANELS = 5
AHEAD = 2
LAYERS = 4


def enter(chip, core, layers=False):
    barrier = pltpu.get_barrier_semaphore()

    def greet(step, carry):
        peer = (chip + step) % CHIPS
        pl.semaphore_signal(barrier, inc=1, device_id={"seq": 2 * peer + core}, device_id_type=MESH)
        return carry

    lax.fori_loop(1, CHIPS, greet, 0)
    pl.semaphore_signal(barrier, inc=1, device_id={"seq": 2 * chip + 1 - core}, device_id_type=MESH)
    if layers:
        layer = lax.axis_index("head")
        for step in (1, LAYERS - 1):
            pl.semaphore_signal(
                barrier, inc=1, device_id={"head": (layer + step) % LAYERS}, device_id_type=MESH
            )
    pl.semaphore_wait(barrier, CHIPS + (2 if layers else 0))


def remote(src, dst, send_sem, recv_sem, device, axis="seq"):
    return pltpu.make_async_remote_copy(
        src_ref=src,
        dst_ref=dst,
        send_sem=send_sem,
        recv_sem=recv_sem,
        device_id={axis: device},
        device_id_type=MESH,
    )


def deal_queries(chip, core, src, dst, send, recv):
    third = third_of(chip)
    slot = chip - start_of(third)
    own_third = chip % 3
    first = start_of(own_third)
    count = start_of(own_third + 1) - first
    partner = 2 * chip + 1 - core

    def copy(h):
        return remote(src.at[h], dst.at[slot], send.at[h], recv.at[slot], 2 * (3 * h + third) + core)

    def own():
        return pltpu.make_async_copy(src.at[chip // 3], dst.at[slot], recv.at[slot])

    def begin():
        def go(h, carry):
            @pl.when(3 * h + third != chip)
            def _():
                copy(h).start()

            @pl.when(3 * h + third == chip)
            def _():
                own().start()

            return carry

        lax.fori_loop(0, HEADS, go, 0)

    def arrived():
        @pl.when(chip < BUSY)
        def _():
            def come(n, carry):
                @pl.when(first + n != chip)
                def _():
                    remote(src.at[0], dst.at[n], send.at[0], recv.at[n], partner).wait_recv()

                @pl.when(first + n == chip)
                def _():
                    own().wait()

                return carry

            lax.fori_loop(0, count, come, 0)

            @pl.when(count < SLOTS)
            def _():
                dst[SLOTS - 1] = jnp.zeros_like(dst[SLOTS - 1])

    def sent():
        def gone(h, carry):
            @pl.when(3 * h + third != chip)
            def _():
                copy(h).wait_send()

            return carry

        lax.fori_loop(0, HEADS, gone, 0)

    return begin, arrived, sent


def deal_keys(chip, core, src, dst, kv_send, kv_recv, pass_send, pass_recv):
    partner = 2 * chip + 1 - core

    def copy(d):
        return remote(src.at[:, d // 3], dst.at[:, chip, core], kv_send.at[d], kv_recv.at[chip], 2 * d + core)

    def own():
        return pltpu.make_async_copy(src.at[:, chip // 3], dst.at[:, chip, core], kv_recv.at[chip])

    def pass_copy(source, half):
        return remote(
            dst.at[:, source, half], dst.at[:, source, half], pass_send.at[source], pass_recv.at[source], partner
        )

    def begin():
        def go(step, carry):
            d = (chip + step) % CHIPS

            @pl.when(jnp.logical_and(d < BUSY, step > 0))
            def _():
                copy(d).start()

            @pl.when(jnp.logical_and(d < BUSY, step == 0))
            def _():
                own().start()

            return carry

        lax.fori_loop(0, CHIPS, go, 0)

    def source_of(step):
        return (chip + CHIPS - step) % CHIPS

    def arrive(step):
        source = source_of(step)

        @pl.when(step > 0)
        def _():
            remote(
                src.at[:, 0], dst.at[:, source, core], kv_send.at[0], kv_recv.at[source], partner
            ).wait_recv()

        @pl.when(step == 0)
        def _():
            own().wait()

        pass_copy(source, core).start()

    def use(step, body):
        source = source_of(step)
        pass_copy(source, 1 - core).wait_recv()
        body(source)

    def consume(body):
        @pl.when(chip < BUSY)
        def _():
            def first(step, carry):
                arrive(step)
                return carry

            def both(step, carry):
                arrive(step)
                use(step - LAG, body)
                return carry

            def last(step, carry):
                use(step, body)
                return carry

            lax.fori_loop(0, LAG, first, 0)
            lax.fori_loop(LAG, CHIPS, both, 0)
            lax.fori_loop(CHIPS - LAG, CHIPS, last, 0)

    def sent():
        @pl.when(chip < BUSY)
        def _():
            def passed(step, carry):
                pass_copy(source_of(step), core).wait_send()
                return carry

            lax.fori_loop(0, CHIPS, passed, 0)

        def gone(step, carry):
            d = (chip + step) % CHIPS

            @pl.when(d < BUSY)
            def _():
                copy(d).wait_send()

            return carry

        lax.fori_loop(1, CHIPS, gone, 0)

    return begin, consume, sent


VMEM = pl.BlockSpec(memory_space=pltpu.VMEM)
HBM = pl.BlockSpec(memory_space=pl.ANY)
DMA = pltpu.SemaphoreType.DMA


class Gather:
    def __init__(self, rows_ref, own_send, pass_send, recv):
        self.ref, self.own_send, self.pass_send, self.recv = rows_ref, own_send, pass_send, recv
        self.layer = lax.axis_index("head")
        self.right, self.left = (self.layer + 1) % LAYERS, (self.layer + LAYERS - 1) % LAYERS
        self.across = (self.layer + 2) % LAYERS
        self.height = rows_ref.shape[0] // LAYERS
        self.width = rows_ref.shape[1] // PANELS

    def rows(self, layer):
        return pl.ds(pl.multiple_of(layer * self.height, self.height), self.height)

    def columns(self, panel):
        return pl.ds(panel * self.width, self.width)

    def block(self, layer, panel):
        return self.ref.at[self.rows(layer), self.columns(panel)]

    def copy(self, layer, panel, send, kind, target):
        block = self.block(layer, panel)
        return remote(block, block, send, self.recv.at[kind, panel], target, "head")

    def own(self, panel):
        return (
            self.copy(self.layer, panel, self.own_send.at[0, panel], 0, self.right),
            self.copy(self.layer, panel, self.own_send.at[1, panel], 1, self.left),
        )

    def start(self, panel):
        for copy in self.own(panel):
            copy.start()

    def passing(self, panel):
        if panel % 2 == 0:
            return self.copy(self.left, panel, self.pass_send.at[panel], 2, self.right)
        return self.copy(self.right, panel, self.pass_send.at[panel], 2, self.left)

    def relay(self, panel):
        if panel % 2 == 0:
            self.copy(self.left, panel, self.pass_send.at[panel], 0, self.right).wait_recv()
        else:
            self.copy(self.right, panel, self.pass_send.at[panel], 1, self.left).wait_recv()
        self.passing(panel).start()

    def rest(self, panel):
        if panel % 2 == 0:
            self.copy(self.right, panel, self.pass_send.at[panel], 1, self.left).wait_recv()
        else:
            self.copy(self.left, panel, self.pass_send.at[panel], 0, self.right).wait_recv()
        self.copy(self.across, panel, self.pass_send.at[panel], 2, self.right).wait_recv()

    def sent(self):
        for panel in range(PANELS):
            for copy in self.own(panel):
                copy.wait_send()
            self.passing(panel).wait_send()


def panel_of_w(w_hbm, w_ref, sems, panel):
    depth = w_ref.shape[1] // PANELS
    rows = pl.ds(panel * depth, depth)
    return pltpu.make_async_copy(w_hbm.at[:, rows], w_ref.at[:, rows], sems.at[panel])


def add_panel(totals, rows_ref, w_ref, panel, first):
    depth = w_ref.shape[1] // PANELS
    span = slice(panel * depth, (panel + 1) * depth)
    for c in range(3):
        term = jnp.dot(rows_ref[:, span], w_ref[c, span, :], preferred_element_type=jnp.float32)
        totals[c] = term if first else totals[c] + term


def split_heads(totals, q_heads, kv_heads):
    for h in range(HEADS):
        span = slice(h * HD, (h + 1) * HD)
        q_heads[h] = totals[0, :, span].astype(jnp.bfloat16)
        kv_heads[0, h] = totals[1, :, span].astype(jnp.bfloat16)
        kv_heads[1, h] = totals[2, :, span].astype(jnp.bfloat16)


def give_back(chip, core, src, dst, send, recv):
    own_third = chip % 3
    first = start_of(own_third)
    count = start_of(own_third + 1) - first
    third = third_of(chip)
    own_head = chip // 3

    def out_copy(n):
        return remote(src.at[n], dst.at[own_head], send.at[n], recv.at[own_head], 2 * (first + n) + core)

    def own():
        return pltpu.make_async_copy(src.at[chip - first], dst.at[own_head], recv.at[own_head])

    def begin():
        @pl.when(chip < BUSY)
        def _():
            def go(n, carry):
                @pl.when(first + n != chip)
                def _():
                    out_copy(n).start()

                @pl.when(first + n == chip)
                def _():
                    own().start()

                return carry

            lax.fori_loop(0, count, go, 0)

    def end():
        def come(h, carry):
            @pl.when(3 * h + third != chip)
            def _():
                remote(src.at[0], dst.at[h], send.at[0], recv.at[h], 2 * chip + 1 - core).wait_recv()

            @pl.when(3 * h + third == chip)
            def _():
                own().wait()

            return carry

        lax.fori_loop(0, HEADS, come, 0)

        @pl.when(chip < BUSY)
        def _():
            def gone(n, carry):
                @pl.when(first + n != chip)
                def _():
                    out_copy(n).wait_send()

                return carry

            lax.fori_loop(0, count, gone, 0)

    return begin, end


TOKENS = 4096
ROWS = SLOTS * HD
CHUNK = 2 * HD
SCALE = HD ** (-0.5)
FACTOR = SCALE * LOG2E


def nt(left, right):
    return lax.dot_general(left, right, (((1,), (1,)), ((), ())), preferred_element_type=jnp.float32)


def nn(left, right):
    return lax.dot_general(left, right, (((1,), (0,)), ((), ())), preferred_element_type=jnp.float32)


def tn(left, right):
    return lax.dot_general(left, right, (((0,), (0,)), ((), ())), preferred_element_type=jnp.float32)


def mask_sides(frames_ref, mask_ref, key_hot, row_bar, barred, first, core):
    frames = frames_ref[...]
    count = mask_ref.shape[0]
    lane = lax.broadcasted_iota(jnp.int32, (1, HD), 1)
    start = jnp.full((1, HD), TOKENS, jnp.int32)
    end = jnp.full((1, HD), TOKENS, jnp.int32)
    for f in range(count):
        below = jnp.sum((frames < f).astype(jnp.float32), keepdims=True).astype(jnp.int32)
        start = jnp.where(lane == f, below, start)
        end = jnp.where(lane == f - 1, below, end)

    def hot(tokens):
        return jnp.where(jnp.logical_and(tokens >= start, tokens < end), 1.0, 0.0).astype(jnp.bfloat16)

    row = lax.broadcasted_iota(jnp.int32, (HD, HD), 0)

    def fill(block, carry):
        key_hot[pl.ds(pl.multiple_of(block * HD, HD), HD), :] = hot(row + block * HD)
        return carry

    lax.fori_loop(0, TOKENS // HD, fill, 0)
    barred[...] = jnp.zeros_like(barred)
    barred[:count, :count] = jnp.where(mask_ref[...] == 1, 0.0, BARRED)
    table = barred[...].astype(jnp.bfloat16)
    for n in range(SLOTS):
        own = hot(row + (2 * (first + n) + core) * HD)
        row_bar[n * HD : (n + 1) * HD, :] = nn(own, table).astype(jnp.bfloat16)


TOP, TOTAL, WEIGHTED, NORM, ROW_DOTS, CURVE = range(6)


def whole_kernel(
    x_ref, w_hbm, readout_ref, frames_ref, mask_ref, gx_ref, pen_ref,
    w_ref, x_all, gx_all, totals, q_heads, kv_heads, r_heads, qd_heads, kvd_heads,
    kv, dots, q, r, qd, key_hot, row_bar, barred, stat,
    dkv, dq_acc, dq, penalty, other, summed, landed, q_landed, p_landed, plain, grads,
    parts, via, direct, mixed, mix_out, kept,
    w_sems, *sems
):
    sems = list(sems)

    def take(n):
        taken = sems[:n]
        del sems[:n]
        return taken

    chip, core = place()
    partner = 2 * chip + 1 - core
    busy = chip < BUSY
    first = start_of(chip % 3)
    for panel in range(PANELS):
        panel_of_w(w_hbm, w_ref, w_sems, panel).start()
    gather = Gather(x_all, *take(3))
    x_all[gather.rows(gather.layer), :] = x_ref[...]
    for h in range(HEADS):
        r_heads[h] = readout_ref[:, h * HD : (h + 1) * HD]
    enter(chip, core, layers=True)
    for panel in range(PANELS):
        gather.start(panel)
    r_begin, r_arrived, r_sent = deal_queries(chip, core, r_heads, r, *take(2))
    q_begin, q_arrived, q_sent = deal_queries(chip, core, q_heads, q, *take(2))
    kv_begin, kv_consume, kv_sent = deal_keys(chip, core, kv_heads, kv, *take(4))
    r_begin()
    mask_sides(frames_ref, mask_ref, key_hot, row_bar, barred, first, core)

    for panel in range(AHEAD):
        gather.relay(panel)
    for panel in range(PANELS):
        if panel + AHEAD < PANELS:
            gather.relay(panel + AHEAD)
        gather.rest(panel)
        panel_of_w(w_hbm, w_ref, w_sems, panel).wait()
        add_panel(totals, x_all, w_ref, panel, panel == 0)
    split_heads(totals, q_heads, kv_heads)
    q_begin()
    kv_begin()

    def keys_of(array, source):
        return array[source].reshape(CHUNK, HD)

    def flat(array):
        return array[...].reshape(ROWS, HD)

    def logits(source):
        hot = key_hot[pl.ds(pl.multiple_of(source * CHUNK, CHUNK), CHUNK), :]
        return nt(
            jnp.concatenate([keys_of(kv.at[0], source), hot], axis=1),
            jnp.concatenate([flat(q), row_bar[...]], axis=1),
        )

    def stats(source):
        raw = logits(source)
        readout_dots = nt(keys_of(kv.at[1], source), flat(r))
        top = stat[TOP]
        new_top = jnp.maximum(top, raw.max(axis=0, keepdims=True))
        weights = jnp.exp2((raw - new_top) * FACTOR)
        shrink = jnp.exp2((top - new_top) * FACTOR)
        stat[TOP] = new_top
        stat[TOTAL] = stat[TOTAL] * shrink + weights.sum(axis=0, keepdims=True)
        stat[WEIGHTED] = stat[WEIGHTED] * shrink + (weights * readout_dots).sum(axis=0, keepdims=True)

    q_arrived()
    r_arrived()

    @pl.when(busy)
    def _():
        stat[...] = jnp.zeros_like(stat)
        stat[TOP] = jnp.full((1, ROWS), BARRED, jnp.float32)
        dq_acc[...] = jnp.zeros_like(dq_acc)

    kv_consume(stats)

    def swap(target):
        x_send, x_recv = swap_sems
        return remote(
            dkv.at[:, target, 1 - core], other.at[:, target], x_send.at[target], x_recv.at[target], partner
        )

    def out_copy(target):
        return remote(
            summed.at[:, target], landed.at[chip], sum_sems[0].at[target], sum_sems[1].at[chip], 2 * target + core
        )

    def own_sum():
        return pltpu.make_async_copy(summed.at[:, chip], landed.at[chip], sum_sems[1].at[chip])

    swap_sems = take(2)
    sum_sems = take(2)
    dq_begin, dq_end = give_back(chip, core, dq, q_landed, *take(2))

    def key_grads(step):
        target = (chip + step) % CHIPS
        weights = jnp.exp2(logits(target) * FACTOR - stat[NORM])
        weights_low = weights.astype(jnp.bfloat16)
        kept[target] = weights_low
        readout_dots = nt(keys_of(kv.at[1], target), flat(r))
        slopes = (weights * (readout_dots - stat[ROW_DOTS])).astype(jnp.bfloat16)
        key_part = (SCALE * nn(slopes, flat(q))).astype(jnp.bfloat16)
        value_part = nn(weights_low, flat(r)).astype(jnp.bfloat16)
        dkv[0, target] = key_part.reshape(2, HD, HD)
        dkv[1, target] = value_part.reshape(2, HD, HD)
        swap(target).start()
        dq_acc[...] += tn(keys_of(kv.at[0], target), slopes)

    def add_partner(step):
        target = (chip + step) % CHIPS
        swap(target).wait_recv()
        summed[:, target] = (
            dkv[:, target, core].astype(jnp.float32) + other[:, target].astype(jnp.float32)
        ).astype(jnp.bfloat16)

        @pl.when(step > 0)
        def _():
            out_copy(target).start()

        @pl.when(step == 0)
        def _():
            own_sum().start()

    @pl.when(busy)
    def _():
        stat[NORM] = stat[TOP] * FACTOR + jnp.log2(stat[TOTAL])
        stat[ROW_DOTS] = stat[WEIGHTED] / stat[TOTAL]
        key_grads(0)

        def go(step, carry):
            key_grads(step)
            add_partner(step - 1)
            return carry

        lax.fori_loop(1, CHIPS, go, 0)
        dq[...] = (SCALE * dq_acc[...]).T.astype(jnp.bfloat16).reshape(SLOTS, HD, HD)

    dq_begin()

    @pl.when(busy)
    def _():
        add_partner(CHIPS - 1)

    gather.sent()
    kv_sent()
    q_sent()
    r_sent()

    def come(step, carry):
        source = (chip + CHIPS - step) % CHIPS

        @pl.when(jnp.logical_and(source < BUSY, step > 0))
        def _():
            remote(
                summed.at[:, 0], landed.at[source], sum_sems[0].at[0], sum_sems[1].at[source], partner
            ).wait_recv()

        @pl.when(jnp.logical_and(source < BUSY, step == 0))
        def _():
            own_sum().wait()

        return carry

    lax.fori_loop(0, CHIPS, come, 0)
    for h in range(HEADS):
        span = slice(h * HD, (h + 1) * HD)
        total = landed[3 * h].astype(jnp.float32) + landed[3 * h + 1].astype(jnp.float32)
        total = (total + landed[3 * h + 2].astype(jnp.float32)).astype(jnp.bfloat16)
        grads[1, :, span] = total[0]
        grads[2, :, span] = total[1]
    dq_end()
    for h in range(HEADS):
        grads[0, :, h * HD : (h + 1) * HD] = q_landed[h]

    regather = Gather(gx_all, *take(3))
    qd_begin, qd_arrived, qd_sent = deal_queries(chip, core, qd_heads, qd, *take(2))
    kvd_begin, kvd_consume, kvd_sent = deal_keys(chip, core, kvd_heads, dots, *take(4))
    via_send, via_recv, direct_send, direct_recv, mix_send, mix_recv = take(6)
    depth = regather.width

    def near_far(panel):
        return (regather.right, regather.left) if panel % 2 == 0 else (regather.left, regather.right)

    def part(layer, panel):
        return parts.at[regather.rows(layer), regather.columns(panel)]

    def piece(ref, panel):
        return ref.at[:, regather.columns(panel)]

    def via_copy(panel):
        return remote(
            part(regather.across, panel), piece(via, panel), via_send.at[panel], via_recv.at[panel],
            near_far(panel)[1], "head",
        )

    def direct_copy(panel):
        target = near_far(panel)[0]
        return remote(
            part(target, panel), piece(direct, panel), direct_send.at[panel], direct_recv.at[panel], target, "head"
        )

    def mix_copy(panel):
        return remote(
            piece(mix_out, panel), piece(mixed, panel), mix_send.at[panel], mix_recv.at[panel],
            near_far(panel)[1], "head",
        )

    def share(panel):
        span = slice(panel * depth, (panel + 1) * depth)
        total = nt(grads[0], w_ref[0, span, :])
        total += nt(grads[1], w_ref[1, span, :])
        total += nt(grads[2], w_ref[2, span, :])
        parts[:, span] = total.astype(jnp.bfloat16)
        via_copy(panel).start()
        direct_copy(panel).start()

    def mix(panel):
        span = slice(panel * depth, (panel + 1) * depth)
        via_copy(panel).wait_recv()
        mine = parts[regather.rows(near_far(panel)[1]), span]
        mix_out[:, span] = (via[:, span].astype(jnp.float32) + mine.astype(jnp.float32)).astype(jnp.bfloat16)
        mix_copy(panel).start()

    def settle(panel):
        span = slice(panel * depth, (panel + 1) * depth)
        direct_copy(panel).wait_recv()
        mix_copy(panel).wait_recv()
        mine = parts[regather.rows(regather.layer), span].astype(jnp.float32)
        total = mine + direct[:, span].astype(jnp.float32) + mixed[:, span].astype(jnp.float32)
        total = total.astype(jnp.bfloat16)
        gx_ref[:, span] = total
        gx_all[regather.rows(regather.layer), span] = total
        regather.start(panel)

    def absorb(panel):
        regather.rest(panel)
        add_panel(totals, gx_all, w_ref, panel, panel == 0)

    stages = ((share, 0), (mix, 2), (settle, 4), (regather.relay, 6), (absorb, 8))
    for step in range(PANELS + stages[-1][1]):
        for stage, lag in stages:
            if 0 <= step - lag < PANELS:
                stage(step - lag)
    split_heads(totals, qd_heads, kvd_heads)
    qd_begin()
    kvd_begin()

    def tangent(source):
        keys, values = keys_of(kv.at[0], source), keys_of(kv.at[1], source)
        key_dots, value_dots = keys_of(dots.at[0], source), keys_of(dots.at[1], source)
        weights_low = kept[source]
        moved = nt(jnp.concatenate([keys, key_dots], axis=1), jnp.concatenate([flat(qd), flat(q)], axis=1))
        turned = weights_low.astype(jnp.float32) * (moved * SCALE)
        dq_acc[...] += tn(values, turned.astype(jnp.bfloat16))
        plain[...] += tn(jnp.concatenate([values, value_dots], axis=1), weights_low)
        stat[CURVE] += turned.sum(axis=0, keepdims=True)

    qd_arrived()

    @pl.when(busy)
    def _():
        dq_acc[...] = jnp.zeros_like(dq_acc)
        plain[...] = jnp.zeros_like(plain)

    kvd_consume(tangent)
    pen_begin, pen_end = give_back(chip, core, penalty, p_landed, *take(2))

    @pl.when(busy)
    def _():
        total = dq_acc[...] + plain[HD:, :] - stat[CURVE] * plain[:HD, :]
        penalty[...] = total.T.astype(jnp.bfloat16).reshape(SLOTS, HD, HD)

    pen_begin()

    @pl.when(busy)
    def _():
        def gone(step, carry):
            target = (chip + step) % CHIPS
            swap(target).wait_send()

            @pl.when(step > 0)
            def _():
                out_copy(target).wait_send()

            return carry

        lax.fori_loop(0, CHIPS, gone, 0)

    regather.sent()
    for panel in range(PANELS):
        via_copy(panel).wait_send()
        direct_copy(panel).wait_send()
        mix_copy(panel).wait_send()
    kvd_sent()
    qd_sent()
    pen_end()
    for h in range(HEADS):
        pen_ref[:, h * HD : (h + 1) * HD] = p_landed[h]


def hand_over_kernel(x_ref, p_ref, x_out, p_out):
    x_out[...] = x_ref[...]
    p_out[...] = p_ref[...]


def hand_over(grad_x, penalty_grad):
    return pl.pallas_call(
        hand_over_kernel,
        out_shape=tuple(jax.ShapeDtypeStruct(a.shape, a.dtype) for a in (grad_x, penalty_grad)),
        in_specs=[VMEM] * 2,
        out_specs=(VMEM, VMEM),
        name="hand_over",
    )(grad_x, penalty_grad)


def on_device(clip_tokens, w_qkv, readout, token_latent_frame, frame_mask):
    panel_rows, width = clip_tokens.shape
    tokens, columns = readout.shape

    def low(*shape):
        return pltpu.VMEM(shape, jnp.bfloat16)

    def wide(*shape):
        return pltpu.VMEM(shape, jnp.float32)

    gather_sems = [DMA((2, PANELS)), DMA((PANELS,)), DMA((3, PANELS))]
    query_sems = [DMA((HEADS,)), DMA((SLOTS,))]
    back_sems = [DMA((SLOTS,)), DMA((HEADS,))]
    chip_sems = [DMA((CHIPS,))] * 4
    scratch = dict(
        w_ref=low(*w_qkv.shape),
        x_all=low(tokens, width),
        gx_all=low(tokens, width),
        totals=wide(3, tokens, columns),
        q_heads=low(HEADS, HD, HD),
        kv_heads=low(2, HEADS, HD, HD),
        r_heads=low(HEADS, HD, HD),
        qd_heads=low(HEADS, HD, HD),
        kvd_heads=low(2, HEADS, HD, HD),
        kv=low(2, CHIPS, 2, HD, HD),
        dots=low(2, CHIPS, 2, HD, HD),
        q=low(SLOTS, HD, HD),
        r=low(SLOTS, HD, HD),
        qd=low(SLOTS, HD, HD),
        key_hot=low(TOKENS, HD),
        row_bar=low(ROWS, HD),
        barred=wide(HD, HD),
        stat=wide(6, 1, ROWS),
        dkv=low(2, CHIPS, 2, HD, HD),
        dq_acc=wide(HD, ROWS),
        dq=low(SLOTS, HD, HD),
        penalty=low(SLOTS, HD, HD),
        other=low(2, CHIPS, HD, HD),
        summed=low(2, CHIPS, HD, HD),
        landed=low(CHIPS, 2, HD, HD),
        q_landed=low(HEADS, HD, HD),
        p_landed=low(HEADS, HD, HD),
        plain=wide(2 * HD, ROWS),
        grads=low(3, tokens, columns),
        parts=low(tokens, width),
        via=low(panel_rows, width),
        direct=low(panel_rows, width),
        mixed=low(panel_rows, width),
        mix_out=low(panel_rows, width),
        kept=low(CHIPS, CHUNK, ROWS),
        w_sems=DMA((PANELS,)),
    )
    sems = (
        gather_sems + query_sems * 2 + chip_sems + chip_sems + back_sems
        + gather_sems + query_sems + chip_sems + [DMA((PANELS,))] * 6 + back_sems
    )
    grad_x, penalty_grad = pl.pallas_call(
        whole_kernel,
        out_shape=(
            jax.ShapeDtypeStruct((panel_rows, width), jnp.bfloat16),
            jax.ShapeDtypeStruct((tokens, columns), jnp.bfloat16),
        ),
        in_specs=[VMEM, HBM, VMEM, VMEM, VMEM],
        out_specs=(VMEM, VMEM),
        scratch_shapes=list(scratch.values()) + sems,
        compiler_params=pltpu.CompilerParams(
            collective_id=0, has_side_effects=True, vmem_limit_bytes=58 << 20
        ),
        name="whole",
    )(clip_tokens, w_qkv, readout, token_latent_frame.reshape(-1, HD), frame_mask)
    return hand_over(grad_x, penalty_grad)


def solution(mesh):
    return jax.shard_map(
        on_device,
        mesh=mesh,
        in_specs=(P(("seq", "head"), None), P(None, None, "head"), P("seq", "head"), P(), P()),
        out_specs=(P(("seq", "head"), None), P("seq", "head")),
        check_vma=False,
    )
```

```python
import functools
import math

import jax
import jax.numpy as jnp
from jax import lax
from jax.experimental import pallas as pl
from jax.experimental.pallas import tpu as pltpu
from jax.sharding import PartitionSpec as P

HD = 128
MESH = pl.DeviceIdType.MESH
LOG2E = math.log2(math.e)
BARRED = -1e30

CHIPS = 16
BUSY = 15
HEADS = 5
SLOTS = 6
LAG = 2


def start_of(third):
    return (CHIPS * third + 2) // 3


def third_of(chip):
    return (chip * 3) // CHIPS


def place():
    me = lax.axis_index("seq")
    return me // 2, me % 2


PANELS = 5
AHEAD = 4
LAYERS = 4


def enter(chip, core, layers=False):
    barrier = pltpu.get_barrier_semaphore()

    def greet(step, carry):
        peer = (chip + step) % CHIPS
        pl.semaphore_signal(barrier, inc=1, device_id={"seq": 2 * peer + core}, device_id_type=MESH)
        return carry

    lax.fori_loop(1, CHIPS, greet, 0)
    pl.semaphore_signal(barrier, inc=1, device_id={"seq": 2 * chip + 1 - core}, device_id_type=MESH)
    if layers:
        layer = lax.axis_index("head")
        for step in (1, LAYERS - 1):
            pl.semaphore_signal(
                barrier, inc=1, device_id={"head": (layer + step) % LAYERS}, device_id_type=MESH
            )
    pl.semaphore_wait(barrier, CHIPS + (2 if layers else 0))


def remote(src, dst, send_sem, recv_sem, device, axis="seq"):
    return pltpu.make_async_remote_copy(
        src_ref=src,
        dst_ref=dst,
        send_sem=send_sem,
        recv_sem=recv_sem,
        device_id={axis: device},
        device_id_type=MESH,
    )


def deal_queries(chip, core, src, dst, send, recv):
    third = third_of(chip)
    slot = chip - start_of(third)
    own_third = chip % 3
    first = start_of(own_third)
    count = start_of(own_third + 1) - first
    partner = 2 * chip + 1 - core

    def copy(h):
        return remote(src.at[h], dst.at[slot], send.at[h], recv.at[slot], 2 * (3 * h + third) + core)

    def own():
        return pltpu.make_async_copy(src.at[chip // 3], dst.at[slot], recv.at[slot])

    def begin():
        def go(h, carry):
            @pl.when(3 * h + third != chip)
            def _():
                copy(h).start()

            @pl.when(3 * h + third == chip)
            def _():
                own().start()

            return carry

        lax.fori_loop(0, HEADS, go, 0)

    def arrived():
        @pl.when(chip < BUSY)
        def _():
            def come(n, carry):
                @pl.when(first + n != chip)
                def _():
                    remote(src.at[0], dst.at[n], send.at[0], recv.at[n], partner).wait_recv()

                @pl.when(first + n == chip)
                def _():
                    own().wait()

                return carry

            lax.fori_loop(0, count, come, 0)

            @pl.when(count < SLOTS)
            def _():
                dst[SLOTS - 1] = jnp.zeros_like(dst[SLOTS - 1])

    def sent():
        def gone(h, carry):
            @pl.when(3 * h + third != chip)
            def _():
                copy(h).wait_send()

            return carry

        lax.fori_loop(0, HEADS, gone, 0)

    return begin, arrived, sent


def deal_keys(chip, core, src, dst, kv_send, kv_recv, pass_send, pass_recv):
    partner = 2 * chip + 1 - core

    def copy(d):
        return remote(src.at[:, d // 3], dst.at[:, chip, core], kv_send.at[d], kv_recv.at[chip], 2 * d + core)

    def own():
        return pltpu.make_async_copy(src.at[:, chip // 3], dst.at[:, chip, core], kv_recv.at[chip])

    def pass_copy(source, half):
        return remote(
            dst.at[:, source, half], dst.at[:, source, half], pass_send.at[source], pass_recv.at[source], partner
        )

    def begin():
        def go(step, carry):
            d = (chip + step) % CHIPS

            @pl.when(jnp.logical_and(d < BUSY, step > 0))
            def _():
                copy(d).start()

            @pl.when(jnp.logical_and(d < BUSY, step == 0))
            def _():
                own().start()

            return carry

        lax.fori_loop(0, CHIPS, go, 0)

    def source_of(step):
        return (chip + CHIPS - step) % CHIPS

    def arrive(step):
        source = source_of(step)

        @pl.when(step > 0)
        def _():
            remote(
                src.at[:, 0], dst.at[:, source, core], kv_send.at[0], kv_recv.at[source], partner
            ).wait_recv()

        @pl.when(step == 0)
        def _():
            own().wait()

        pass_copy(source, core).start()

    def use(step, body):
        source = source_of(step)
        pass_copy(source, 1 - core).wait_recv()
        body(source)

    def consume(body):
        @pl.when(chip < BUSY)
        def _():
            def first(step, carry):
                arrive(step)
                return carry

            def both(step, carry):
                arrive(step)
                use(step - LAG, body)
                return carry

            def last(step, carry):
                use(step, body)
                return carry

            lax.fori_loop(0, LAG, first, 0)
            lax.fori_loop(LAG, CHIPS, both, 0)
            lax.fori_loop(CHIPS - LAG, CHIPS, last, 0)

    def sent():
        @pl.when(chip < BUSY)
        def _():
            def passed(step, carry):
                pass_copy(source_of(step), core).wait_send()
                return carry

            lax.fori_loop(0, CHIPS, passed, 0)

        def gone(step, carry):
            d = (chip + step) % CHIPS

            @pl.when(d < BUSY)
            def _():
                copy(d).wait_send()

            return carry

        lax.fori_loop(1, CHIPS, gone, 0)

    return begin, consume, sent


VMEM = pl.BlockSpec(memory_space=pltpu.VMEM)
HBM = pl.BlockSpec(memory_space=pl.ANY)
DMA = pltpu.SemaphoreType.DMA


class Gather:
    def __init__(self, rows_ref, own_send, pass_send, recv):
        self.ref, self.own_send, self.pass_send, self.recv = rows_ref, own_send, pass_send, recv
        self.layer = lax.axis_index("head")
        self.right, self.left = (self.layer + 1) % LAYERS, (self.layer + LAYERS - 1) % LAYERS
        self.across = (self.layer + 2) % LAYERS
        self.height = rows_ref.shape[0] // LAYERS
        self.width = rows_ref.shape[1] // PANELS

    def rows(self, layer):
        return pl.ds(pl.multiple_of(layer * self.height, self.height), self.height)

    def columns(self, panel):
        return pl.ds(panel * self.width, self.width)

    def block(self, layer, panel):
        return self.ref.at[self.rows(layer), self.columns(panel)]

    def copy(self, layer, panel, send, kind, target):
        block = self.block(layer, panel)
        return remote(block, block, send, self.recv.at[kind, panel], target, "head")

    def own(self, panel):
        return (
            self.copy(self.layer, panel, self.own_send.at[0, panel], 0, self.right),
            self.copy(self.layer, panel, self.own_send.at[1, panel], 1, self.left),
        )

    def start(self, panel):
        for copy in self.own(panel):
            copy.start()

    def passing(self, panel):
        if panel % 2 == 0:
            return self.copy(self.left, panel, self.pass_send.at[panel], 2, self.right)
        return self.copy(self.right, panel, self.pass_send.at[panel], 2, self.left)

    def relay(self, panel):
        if panel % 2 == 0:
            self.copy(self.left, panel, self.pass_send.at[panel], 0, self.right).wait_recv()
        else:
            self.copy(self.right, panel, self.pass_send.at[panel], 1, self.left).wait_recv()
        self.passing(panel).start()

    def rest(self, panel):
        if panel % 2 == 0:
            self.copy(self.right, panel, self.pass_send.at[panel], 1, self.left).wait_recv()
        else:
            self.copy(self.left, panel, self.pass_send.at[panel], 0, self.right).wait_recv()
        self.copy(self.across, panel, self.pass_send.at[panel], 2, self.right).wait_recv()

    def sent(self):
        for panel in range(PANELS):
            for copy in self.own(panel):
                copy.wait_send()
            self.passing(panel).wait_send()


def panel_of_w(w_hbm, w_ref, sems, panel):
    depth = w_ref.shape[1] // PANELS
    rows = pl.ds(panel * depth, depth)
    return pltpu.make_async_copy(w_hbm.at[:, rows], w_ref.at[:, rows], sems.at[panel])


def add_panel(totals, rows_ref, w_ref, panel, first):
    depth = w_ref.shape[1] // PANELS
    span = slice(panel * depth, (panel + 1) * depth)
    for c in range(3):
        term = jnp.dot(rows_ref[:, span], w_ref[c, span, :], preferred_element_type=jnp.float32)
        totals[c] = term if first else totals[c] + term


def split_heads(totals, q_heads, kv_heads):
    for h in range(HEADS):
        span = slice(h * HD, (h + 1) * HD)
        q_heads[h] = totals[0, :, span].astype(jnp.bfloat16)
        kv_heads[0, h] = totals[1, :, span].astype(jnp.bfloat16)
        kv_heads[1, h] = totals[2, :, span].astype(jnp.bfloat16)


def give_back(chip, core, src, dst, send, recv):
    own_third = chip % 3
    first = start_of(own_third)
    count = start_of(own_third + 1) - first
    third = third_of(chip)
    own_head = chip // 3

    def out_copy(n):
        return remote(src.at[n], dst.at[own_head], send.at[n], recv.at[own_head], 2 * (first + n) + core)

    def own():
        return pltpu.make_async_copy(src.at[chip - first], dst.at[own_head], recv.at[own_head])

    def begin():
        @pl.when(chip < BUSY)
        def _():
            def go(n, carry):
                @pl.when(first + n != chip)
                def _():
                    out_copy(n).start()

                @pl.when(first + n == chip)
                def _():
                    own().start()

                return carry

            lax.fori_loop(0, count, go, 0)

    def end():
        def come(h, carry):
            @pl.when(3 * h + third != chip)
            def _():
                remote(src.at[0], dst.at[h], send.at[0], recv.at[h], 2 * chip + 1 - core).wait_recv()

            @pl.when(3 * h + third == chip)
            def _():
                own().wait()

            return carry

        lax.fori_loop(0, HEADS, come, 0)

        @pl.when(chip < BUSY)
        def _():
            def gone(n, carry):
                @pl.when(first + n != chip)
                def _():
                    out_copy(n).wait_send()

                return carry

            lax.fori_loop(0, count, gone, 0)

    return begin, end


TOKENS = 4096
ROWS = SLOTS * HD
CHUNK = 2 * HD
SCALE = HD ** (-0.5)
FACTOR = SCALE * LOG2E


def nt(left, right):
    return lax.dot_general(left, right, (((1,), (1,)), ((), ())), preferred_element_type=jnp.float32)


def nn(left, right):
    return lax.dot_general(left, right, (((1,), (0,)), ((), ())), preferred_element_type=jnp.float32)


def tn(left, right):
    return lax.dot_general(left, right, (((0,), (0,)), ((), ())), preferred_element_type=jnp.float32)


def mask_sides(frames_ref, mask_ref, key_hot, row_bar, barred, first, core):
    frames = frames_ref[...]
    count = mask_ref.shape[0]
    lane = lax.broadcasted_iota(jnp.int32, (1, HD), 1)
    start = jnp.full((1, HD), TOKENS, jnp.int32)
    end = jnp.full((1, HD), TOKENS, jnp.int32)
    for f in range(count):
        below = jnp.sum((frames < f).astype(jnp.float32), keepdims=True).astype(jnp.int32)
        start = jnp.where(lane == f, below, start)
        end = jnp.where(lane == f - 1, below, end)

    def hot(tokens):
        return jnp.where(jnp.logical_and(tokens >= start, tokens < end), 1.0, 0.0).astype(jnp.bfloat16)

    row = lax.broadcasted_iota(jnp.int32, (HD, HD), 0)

    def fill(block, carry):
        key_hot[pl.ds(pl.multiple_of(block * HD, HD), HD), :] = hot(row + block * HD)
        return carry

    lax.fori_loop(0, TOKENS // HD, fill, 0)
    barred[...] = jnp.zeros_like(barred)
    barred[:count, :count] = jnp.where(mask_ref[...] == 1, 0.0, BARRED)
    table = barred[...].astype(jnp.bfloat16)
    for n in range(SLOTS):
        own = hot(row + (2 * (first + n) + core) * HD)
        row_bar[n * HD : (n + 1) * HD, :] = nn(own, table).astype(jnp.bfloat16)


TOP, TOTAL, WEIGHTED, NORM, ROW_DOTS, CURVE = range(6)


def whole_kernel(
    x_ref, w_hbm, readout_ref, frames_ref, mask_ref, gx_ref, pen_ref,
    w_ref, x_all, gx_all, totals, q_heads, kv_heads, r_heads, qd_heads, kvd_heads,
    kv, dots, q, r, qd, key_hot, row_bar, barred, stat,
    dkv, dq_acc, dq, penalty, other, summed, landed, q_landed, p_landed, plain, grads,
    parts, via, direct, mixed, mix_out, kept,
    w_sems, *sems
):
    sems = list(sems)

    def take(n):
        taken = sems[:n]
        del sems[:n]
        return taken

    chip, core = place()
    partner = 2 * chip + 1 - core
    busy = chip < BUSY
    first = start_of(chip % 3)
    for panel in range(PANELS):
        panel_of_w(w_hbm, w_ref, w_sems, panel).start()
    gather = Gather(x_all, *take(3))
    x_all[gather.rows(gather.layer), :] = x_ref[...]
    for h in range(HEADS):
        r_heads[h] = readout_ref[:, h * HD : (h + 1) * HD]
    enter(chip, core, layers=True)
    for panel in range(PANELS):
        gather.start(panel)
    r_begin, r_arrived, r_sent = deal_queries(chip, core, r_heads, r, *take(2))
    q_begin, q_arrived, q_sent = deal_queries(chip, core, q_heads, q, *take(2))
    kv_begin, kv_consume, kv_sent = deal_keys(chip, core, kv_heads, kv, *take(4))
    r_begin()
    mask_sides(frames_ref, mask_ref, key_hot, row_bar, barred, first, core)

    for panel in range(AHEAD):
        gather.relay(panel)
    for panel in range(PANELS):
        if panel + AHEAD < PANELS:
            gather.relay(panel + AHEAD)
        gather.rest(panel)
        panel_of_w(w_hbm, w_ref, w_sems, panel).wait()
        add_panel(totals, x_all, w_ref, panel, panel == 0)
    split_heads(totals, q_heads, kv_heads)
    q_begin()
    kv_begin()

    def keys_of(array, source):
        return array[source].reshape(CHUNK, HD)

    def flat(array):
        return array[...].reshape(ROWS, HD)

    def logits(source):
        hot = key_hot[pl.ds(pl.multiple_of(source * CHUNK, CHUNK), CHUNK), :]
        return nt(
            jnp.concatenate([keys_of(kv.at[0], source), hot], axis=1),
            jnp.concatenate([flat(q), row_bar[...]], axis=1),
        )

    def stats(source):
        raw = logits(source)
        readout_dots = nt(keys_of(kv.at[1], source), flat(r))
        top = stat[TOP]
        new_top = jnp.maximum(top, raw.max(axis=0, keepdims=True))
        weights = jnp.exp2((raw - new_top) * FACTOR)
        shrink = jnp.exp2((top - new_top) * FACTOR)
        stat[TOP] = new_top
        stat[TOTAL] = stat[TOTAL] * shrink + weights.sum(axis=0, keepdims=True)
        stat[WEIGHTED] = stat[WEIGHTED] * shrink + (weights * readout_dots).sum(axis=0, keepdims=True)

    q_arrived()
    r_arrived()

    @pl.when(busy)
    def _():
        stat[...] = jnp.zeros_like(stat)
        stat[TOP] = jnp.full((1, ROWS), BARRED, jnp.float32)
        dq_acc[...] = jnp.zeros_like(dq_acc)

    kv_consume(stats)

    def swap(target):
        x_send, x_recv = swap_sems
        return remote(
            dkv.at[:, target, 1 - core], other.at[:, target], x_send.at[target], x_recv.at[target], partner
        )

    def out_copy(target):
        return remote(
            summed.at[:, target], landed.at[chip], sum_sems[0].at[target], sum_sems[1].at[chip], 2 * target + core
        )

    def own_sum():
        return pltpu.make_async_copy(summed.at[:, chip], landed.at[chip], sum_sems[1].at[chip])

    swap_sems = take(2)
    sum_sems = take(2)
    dq_begin, dq_end = give_back(chip, core, dq, q_landed, *take(2))

    def key_grads(step):
        target = (chip + step) % CHIPS
        weights = jnp.exp2(logits(target) * FACTOR - stat[NORM])
        weights_low = weights.astype(jnp.bfloat16)
        kept[target] = weights_low
        readout_dots = nt(keys_of(kv.at[1], target), flat(r))
        slopes = (weights * (readout_dots - stat[ROW_DOTS])).astype(jnp.bfloat16)
        key_part = (SCALE * nn(slopes, flat(q))).astype(jnp.bfloat16)
        value_part = nn(weights_low, flat(r)).astype(jnp.bfloat16)
        dkv[0, target] = key_part.reshape(2, HD, HD)
        dkv[1, target] = value_part.reshape(2, HD, HD)
        swap(target).start()
        dq_acc[...] += tn(keys_of(kv.at[0], target), slopes)

    def add_partner(step):
        target = (chip + step) % CHIPS
        swap(target).wait_recv()
        summed[:, target] = (
            dkv[:, target, core].astype(jnp.float32) + other[:, target].astype(jnp.float32)
        ).astype(jnp.bfloat16)

        @pl.when(step > 0)
        def _():
            out_copy(target).start()

        @pl.when(step == 0)
        def _():
            own_sum().start()

    @pl.when(busy)
    def _():
        stat[NORM] = stat[TOP] * FACTOR + jnp.log2(stat[TOTAL])
        stat[ROW_DOTS] = stat[WEIGHTED] / stat[TOTAL]
        key_grads(0)

        def go(step, carry):
            key_grads(step)
            add_partner(step - 1)
            return carry

        lax.fori_loop(1, CHIPS, go, 0)
        dq[...] = (SCALE * dq_acc[...]).T.astype(jnp.bfloat16).reshape(SLOTS, HD, HD)

    dq_begin()

    @pl.when(busy)
    def _():
        add_partner(CHIPS - 1)

    gather.sent()
    kv_sent()
    q_sent()
    r_sent()

    def come(step, carry):
        source = (chip + CHIPS - step) % CHIPS

        @pl.when(jnp.logical_and(source < BUSY, step > 0))
        def _():
            remote(
                summed.at[:, 0], landed.at[source], sum_sems[0].at[0], sum_sems[1].at[source], partner
            ).wait_recv()

        @pl.when(jnp.logical_and(source < BUSY, step == 0))
        def _():
            own_sum().wait()

        return carry

    lax.fori_loop(0, CHIPS, come, 0)
    for h in range(HEADS):
        span = slice(h * HD, (h + 1) * HD)
        total = landed[3 * h].astype(jnp.float32) + landed[3 * h + 1].astype(jnp.float32)
        total = (total + landed[3 * h + 2].astype(jnp.float32)).astype(jnp.bfloat16)
        grads[1, :, span] = total[0]
        grads[2, :, span] = total[1]
    dq_end()
    for h in range(HEADS):
        grads[0, :, h * HD : (h + 1) * HD] = q_landed[h]

    regather = Gather(gx_all, *take(3))
    qd_begin, qd_arrived, qd_sent = deal_queries(chip, core, qd_heads, qd, *take(2))
    kvd_begin, kvd_consume, kvd_sent = deal_keys(chip, core, kvd_heads, dots, *take(4))
    via_send, via_recv, direct_send, direct_recv, mix_send, mix_recv = take(6)
    depth = regather.width

    def near_far(panel):
        return (regather.right, regather.left) if panel % 2 == 0 else (regather.left, regather.right)

    def part(layer, panel):
        return parts.at[regather.rows(layer), regather.columns(panel)]

    def piece(ref, panel):
        return ref.at[:, regather.columns(panel)]

    def via_copy(panel):
        return remote(
            part(regather.across, panel), piece(via, panel), via_send.at[panel], via_recv.at[panel],
            near_far(panel)[1], "head",
        )

    def direct_copy(panel):
        target = near_far(panel)[0]
        return remote(
            part(target, panel), piece(direct, panel), direct_send.at[panel], direct_recv.at[panel], target, "head"
        )

    def mix_copy(panel):
        return remote(
            piece(mix_out, panel), piece(mixed, panel), mix_send.at[panel], mix_recv.at[panel],
            near_far(panel)[1], "head",
        )

    def share(panel):
        span = slice(panel * depth, (panel + 1) * depth)
        total = nt(grads[0], w_ref[0, span, :])
        total += nt(grads[1], w_ref[1, span, :])
        total += nt(grads[2], w_ref[2, span, :])
        parts[:, span] = total.astype(jnp.bfloat16)
        via_copy(panel).start()
        direct_copy(panel).start()

    def mix(panel):
        span = slice(panel * depth, (panel + 1) * depth)
        via_copy(panel).wait_recv()
        mine = parts[regather.rows(near_far(panel)[1]), span]
        mix_out[:, span] = (via[:, span].astype(jnp.float32) + mine.astype(jnp.float32)).astype(jnp.bfloat16)
        mix_copy(panel).start()

    def settle(panel):
        span = slice(panel * depth, (panel + 1) * depth)
        direct_copy(panel).wait_recv()
        mix_copy(panel).wait_recv()
        mine = parts[regather.rows(regather.layer), span].astype(jnp.float32)
        total = mine + direct[:, span].astype(jnp.float32) + mixed[:, span].astype(jnp.float32)
        total = total.astype(jnp.bfloat16)
        gx_ref[:, span] = total
        gx_all[regather.rows(regather.layer), span] = total
        regather.start(panel)

    def absorb(panel):
        regather.rest(panel)
        add_panel(totals, gx_all, w_ref, panel, panel == 0)

    stages = ((share, 0), (mix, 2), (settle, 4), (regather.relay, 6), (absorb, 8))
    for step in range(PANELS + stages[-1][1]):
        for stage, lag in stages:
            if 0 <= step - lag < PANELS:
                stage(step - lag)
    split_heads(totals, qd_heads, kvd_heads)
    qd_begin()
    kvd_begin()

    def tangent(source):
        keys, values = keys_of(kv.at[0], source), keys_of(kv.at[1], source)
        key_dots, value_dots = keys_of(dots.at[0], source), keys_of(dots.at[1], source)
        weights_low = kept[source]
        moved = nt(jnp.concatenate([keys, key_dots], axis=1), jnp.concatenate([flat(qd), flat(q)], axis=1))
        turned = weights_low.astype(jnp.float32) * (moved * SCALE)
        dq_acc[...] += tn(values, turned.astype(jnp.bfloat16))
        plain[...] += tn(jnp.concatenate([values, value_dots], axis=1), weights_low)
        stat[CURVE] += turned.sum(axis=0, keepdims=True)

    qd_arrived()

    @pl.when(busy)
    def _():
        dq_acc[...] = jnp.zeros_like(dq_acc)
        plain[...] = jnp.zeros_like(plain)

    kvd_consume(tangent)
    pen_begin, pen_end = give_back(chip, core, penalty, p_landed, *take(2))

    @pl.when(busy)
    def _():
        total = dq_acc[...] + plain[HD:, :] - stat[CURVE] * plain[:HD, :]
        penalty[...] = total.T.astype(jnp.bfloat16).reshape(SLOTS, HD, HD)

    pen_begin()

    @pl.when(busy)
    def _():
        def gone(step, carry):
            target = (chip + step) % CHIPS
            swap(target).wait_send()

            @pl.when(step > 0)
            def _():
                out_copy(target).wait_send()

            return carry

        lax.fori_loop(0, CHIPS, gone, 0)

    regather.sent()
    for panel in range(PANELS):
        via_copy(panel).wait_send()
        direct_copy(panel).wait_send()
        mix_copy(panel).wait_send()
    kvd_sent()
    qd_sent()
    pen_end()
    for h in range(HEADS):
        pen_ref[:, h * HD : (h + 1) * HD] = p_landed[h]


def hand_over_kernel(x_ref, p_ref, x_out, p_out):
    x_out[...] = x_ref[...]
    p_out[...] = p_ref[...]


def hand_over(grad_x, penalty_grad):
    return pl.pallas_call(
        hand_over_kernel,
        out_shape=tuple(jax.ShapeDtypeStruct(a.shape, a.dtype) for a in (grad_x, penalty_grad)),
        in_specs=[VMEM] * 2,
        out_specs=(VMEM, VMEM),
        name="hand_over",
    )(grad_x, penalty_grad)


def on_device(clip_tokens, w_qkv, readout, token_latent_frame, frame_mask):
    panel_rows, width = clip_tokens.shape
    tokens, columns = readout.shape

    def low(*shape):
        return pltpu.VMEM(shape, jnp.bfloat16)

    def wide(*shape):
        return pltpu.VMEM(shape, jnp.float32)

    gather_sems = [DMA((2, PANELS)), DMA((PANELS,)), DMA((3, PANELS))]
    query_sems = [DMA((HEADS,)), DMA((SLOTS,))]
    back_sems = [DMA((SLOTS,)), DMA((HEADS,))]
    chip_sems = [DMA((CHIPS,))] * 4
    scratch = dict(
        w_ref=low(*w_qkv.shape),
        x_all=low(tokens, width),
        gx_all=low(tokens, width),
        totals=wide(3, tokens, columns),
        q_heads=low(HEADS, HD, HD),
        kv_heads=low(2, HEADS, HD, HD),
        r_heads=low(HEADS, HD, HD),
        qd_heads=low(HEADS, HD, HD),
        kvd_heads=low(2, HEADS, HD, HD),
        kv=low(2, CHIPS, 2, HD, HD),
        dots=low(2, CHIPS, 2, HD, HD),
        q=low(SLOTS, HD, HD),
        r=low(SLOTS, HD, HD),
        qd=low(SLOTS, HD, HD),
        key_hot=low(TOKENS, HD),
        row_bar=low(ROWS, HD),
        barred=wide(HD, HD),
        stat=wide(6, 1, ROWS),
        dkv=low(2, CHIPS, 2, HD, HD),
        dq_acc=wide(HD, ROWS),
        dq=low(SLOTS, HD, HD),
        penalty=low(SLOTS, HD, HD),
        other=low(2, CHIPS, HD, HD),
        summed=low(2, CHIPS, HD, HD),
        landed=low(CHIPS, 2, HD, HD),
        q_landed=low(HEADS, HD, HD),
        p_landed=low(HEADS, HD, HD),
        plain=wide(2 * HD, ROWS),
        grads=low(3, tokens, columns),
        parts=low(tokens, width),
        via=low(panel_rows, width),
        direct=low(panel_rows, width),
        mixed=low(panel_rows, width),
        mix_out=low(panel_rows, width),
        kept=low(CHIPS, CHUNK, ROWS),
        w_sems=DMA((PANELS,)),
    )
    sems = (
        gather_sems + query_sems * 2 + chip_sems + chip_sems + back_sems
        + gather_sems + query_sems + chip_sems + [DMA((PANELS,))] * 6 + back_sems
    )
    grad_x, penalty_grad = pl.pallas_call(
        whole_kernel,
        out_shape=(
            jax.ShapeDtypeStruct((panel_rows, width), jnp.bfloat16),
            jax.ShapeDtypeStruct((tokens, columns), jnp.bfloat16),
        ),
        in_specs=[VMEM, HBM, VMEM, VMEM, VMEM],
        out_specs=(VMEM, VMEM),
        scratch_shapes=list(scratch.values()) + sems,
        compiler_params=pltpu.CompilerParams(
            collective_id=0, has_side_effects=True, vmem_limit_bytes=58 << 20
        ),
        name="whole",
    )(clip_tokens, w_qkv, readout, token_latent_frame.reshape(-1, HD), frame_mask)
    return hand_over(grad_x, penalty_grad)


def solution(mesh):
    return jax.shard_map(
        on_device,
        mesh=mesh,
        in_specs=(P(("seq", "head"), None), P(None, None, "head"), P("seq", "head"), P(), P()),
        out_specs=(P(("seq", "head"), None), P("seq", "head")),
        check_vma=False,
    )
```
